128 devices in a mesh: row: 8 (over z, x_lo), col: 16 (over x_hi, y, core).
Axes of the slice: x: 4 (x_hi: 2, x_lo: 2; x = x_hi * 2 + x_lo), y: 4, z: 4, core: 2. Of those that a mesh axis runs over, the one named last changes fastest.
Arguments:
- integrals: bfloat16 [12800, 6400], P(None, 'col'), may hold values from -0.109375 to 0.109375
- packed_store: bfloat16 [9216, 50, 50], P(('row', 'col')), may hold values from -6 to 6
- pair_sector: int32 [6400], replicated, may hold values from 0 to 1
- owner_map: int32 [128], replicated, may hold values from 0 to 127, each once
Outputs:
- cycle_term: bfloat16 [12800, 6400], P('col', 'row')
The draws below stay inside these ranges and needn't reach their ends.
Inputs may be any that keep to these rules, and one draw needn't show every extreme that they name: owner_map is a permutation of the devices.
All inputs are finite; a program needn't handle non-finite values.
Results may differ from the reference program's by a relative error of at most 0.001.
Values may be sent and summed in bfloat16 or wider, within the bound.
A program may use at most 192 MiB of HBM per device.

```python
import jax
import jax.numpy as jnp

BS = 50
NIRREP = 2
NB = 128
NP = 6400
R = 12800
SLOTS = 72
N_ROW = 8
N_COL = 16
DEVICES = 128


def touch_ends(array, rng, least, high):
    longest = array.shape.index(max(array.shape))
    spots = []
    for shift in (0, 1):
        where = [jax.random.randint(jax.random.fold_in(rng, axis), (), 0, length) for axis, length in enumerate(array.shape)]
        where[longest] = (where[longest] + shift) % array.shape[longest]
        spots.append(tuple(where))
    return array.at[spots[0]].set(least).at[spots[1]].set(high)


def with_spikes(drawn, key, source, target, shards_of, factor):
    def block_of(dim):
        return (jnp.arange(drawn.shape[dim]) // (drawn.shape[dim] // shards_of)).reshape((-1,) + (1,) * (drawn.ndim - 1 - dim))

    one_side = jax.random.permutation(key, shards_of)[block_of(target)]
    far = (block_of(target) + shards_of // 2) % shards_of
    return jnp.where((block_of(source) == one_side) | (block_of(source) == far), factor * drawn, drawn)


def steps_of(own_key, dims, shards, low, high):
    level = 1.0
    for position, blocks in shards:
        heights = jax.random.uniform(jax.random.fold_in(jax.random.fold_in(own_key, 6), position), (blocks,), jnp.float32, low / len(shards), high / len(shards))
        level = level * jnp.repeat(jnp.exp(heights), dims[position] // blocks).reshape((-1,) + (1,) * (len(dims) - 1 - position))
    return level


def scatter_about(own_key, extent, deviation, bound, split=(), kind=jnp.bfloat16):
    values = jax.random.normal(own_key, extent, jnp.float32) * deviation
    if len(split) > 0:
        values = steps_of(own_key, extent, split, -0.22, 0.18) * values
    return jnp.clip(values, min=-bound, max=bound).astype(kind)


def gaussian_with(key, shape, width, bound, split, heavy, kind=jnp.bfloat16):
    drawn = width * jax.random.normal(key, shape, jnp.float32)
    if split:
        drawn = drawn * steps_of(key, shape, split, -0.22, 0.18)
    return jnp.clip(with_spikes(drawn, jax.random.fold_in(key, 3), *heavy), -bound, bound).astype(kind)


def setup_inputs(seed: int = 0) -> dict:
    key_of = jax.random.split(jax.random.key(seed), 5)
    integrals = gaussian_with(key_of[0], (R, NP), NP ** -0.5, 0.109375, ((1, 16),), (1, 0, 16, 2.0))
    packed_store = scatter_about(key_of[1], (DEVICES * SLOTS, BS, BS), 1.0, 6.0, ((0, 128),))
    pair_sector = touch_ends(jax.random.randint(key_of[2], (NP,), 0, NIRREP), jax.random.fold_in(key_of[2], 1), 0, NIRREP - 1).astype(jnp.int32)
    owner_map = jax.random.permutation(key_of[3], DEVICES).astype(jnp.int32)
    return dict(integrals=integrals, packed_store=packed_store, pair_sector=pair_sector, owner_map=owner_map)


def packed_positions(owner_map, row_devices, col_devices, slot_count):
    block_total = row_devices * col_devices
    local_row = jnp.arange(row_devices, dtype=jnp.int32)[:, None, None, None]
    local_col = jnp.arange(col_devices, dtype=jnp.int32)[None, :, None, None]
    tile_down = jnp.arange(col_devices, dtype=jnp.int32)[None, None, :, None]
    tile_across = jnp.arange(row_devices, dtype=jnp.int32)[None, None, None, :]
    is_upper = (row_devices * tile_down + local_row <= col_devices * tile_across + local_col).astype(jnp.int32)
    flat_upper = is_upper.reshape(row_devices, col_devices, col_devices * row_devices)
    rank_table = (jnp.cumsum(flat_upper, axis=2) - flat_upper).astype(jnp.int32)
    rank_table = rank_table.reshape(row_devices, col_devices, col_devices, row_devices)
    block_rows = jnp.arange(block_total, dtype=jnp.int32)[:, None]
    block_cols = jnp.arange(block_total, dtype=jnp.int32)[None, :]
    lower_end = jnp.minimum(block_rows, block_cols)
    upper_end = jnp.maximum(block_rows, block_cols)
    class_row = lower_end % row_devices
    class_col = upper_end % col_devices
    slot_index = rank_table[class_row, class_col, lower_end // row_devices, upper_end // col_devices]
    owner_index = owner_map[class_row * col_devices + class_col]
    return (owner_index * slot_count + slot_index).astype(jnp.int32)


def reference(integrals, packed_store, pair_sector, owner_map):
    positions = packed_positions(owner_map, N_ROW, N_COL, SLOTS)
    blocks = packed_store[positions]
    flipped = jnp.swapaxes(blocks, 2, 3)
    inner_rows = jnp.arange(BS, dtype=jnp.int32)[None, None, :, None]
    inner_cols = jnp.arange(BS, dtype=jnp.int32)[None, None, None, :]
    mirrored = jnp.where(inner_rows <= inner_cols, blocks, flipped)
    outer_rows = jnp.arange(NB, dtype=jnp.int32)[:, None, None, None]
    outer_cols = jnp.arange(NB, dtype=jnp.int32)[None, :, None, None]
    chosen = jnp.where(outer_rows < outer_cols, blocks, jnp.where(outer_rows > outer_cols, flipped, mirrored))
    amplitude = chosen.transpose(0, 2, 1, 3).reshape(NP, NP)
    same_sector = pair_sector[:, None] == pair_sector[None, :]
    amplitude = jnp.where(same_sector, amplitude, jnp.zeros((), jnp.bfloat16))
    return jnp.dot(integrals, amplitude, preferred_element_type=jnp.float32).astype(jnp.bfloat16)
```

```python
import jax
import jax.numpy as jnp
from jax import lax
from jax.experimental import pallas as pl
from jax.experimental.pallas import tpu as pltpu
from jax.sharding import PartitionSpec as P

MESH = pl.DeviceIdType.MESH
BF = jnp.bfloat16
F32 = jnp.float32

TILE = 800
KB = 400
MAIN = 384
REM = 16
PIECE = 208
SLOT = PIECE + REM
ROWS = 4 * SLOT
NPAD = 896
OFFS = [(0, 1), (0, 3), (1, 1), (1, 3), (0, 2), (1, 2)]


def piece_start(q):
    return 192 * q + 16 * (q // 3)


def kernel(slots, owner, integrals, packed, mask, out,
           sendbuf, mid, fin, rem_in, stage, stage_full, irecv, arecv,
           x_buf, e1, e2, s_buf, st_buf, acc, l_buf, arem,
           lsem, rsem, s1_send, s1_recv, s2_send, s2_recv, p1_send, p1_recv, full_send, full_recv,
           z_send, z_recv, z2_send, z2_recv, ex_send, ex_recv, a_send, a_recv):
    r = lax.axis_index("row")
    c = lax.axis_index("col")
    z, xl = r // 2, r % 2
    xh, y, k = c // 8, (c // 2) % 4, c % 2

    def col(xh_, y_, k_):
        return xh_ * 8 + (y_ % 4) * 2 + k_

    def remote(src, dst, ssem, rsem_, row_, col_):
        return pltpu.make_async_remote_copy(src_ref=src, dst_ref=dst, send_sem=ssem, recv_sem=rsem_,
                                            device_id=(row_, col_), device_id_type=MESH)

    sends = []

    def send(cp):
        cp.start()
        sends.append(cp)

    mate = c + 1 - 2 * k
    cross_c = c + 8 - 16 * xh
    row_flip = z * 2 + 1 - xl

    local = []

    def fetch(i, cc, q, dst):
        start = pl.multiple_of(cc * TILE + piece_start(q), 16)
        a = pltpu.make_async_copy(integrals.at[pl.ds(start, PIECE), pl.ds(0, MAIN)], dst, lsem.at[i])
        b = pltpu.make_async_copy(integrals.at[pl.ds(start, PIECE), pl.ds(MAIN, REM)], rem_in.at[i], rsem.at[i])
        a.start()
        b.start()
        local.append((a, b))

    n = 0
    for o, (dxh, dy) in enumerate(OFFS):
        for kk in range(2):
            cc = col(xh + dxh - 2 * xh * dxh, y + dy, kk)
            fetch(n, cc, z, stage.at[n, pl.ds(0, PIECE), :])
            n += 1
    full_c = [mate, col(1 - xh, y, 0), col(1 - xh, y, 1)]
    for f in range(3):
        for q in range(4):
            fetch(n, full_c[f], q, stage_full.at[f, pl.ds(q * SLOT, PIECE), :])
            n += 1
    for q in range(4):
        fetch(n, c, q, irecv.at[c, pl.ds(q * SLOT, PIECE), :])
        n += 1

    for cc in range(16):
        def pick(rr, carry):
            sendbuf[cc, rr] = packed[slots[rr * 16 + cc]]
            return carry
        lax.fori_loop(0, 8, pick, 0, unroll=True)
    for d in range(1, 16):
        cc = (c + d) % 16
        send(remote(sendbuf.at[cc], mid.at[:, c], s1_send.at[d], s1_recv.at[d], r, cc))
    own1 = pltpu.make_async_copy(sendbuf.at[c], mid.at[:, c], s1_send.at[0])
    own1.start()

    eye = (lax.broadcasted_iota(jnp.int32, (REM, REM), 0) == lax.broadcasted_iota(jnp.int32, (REM, REM), 1)).astype(BF)

    def add_rem(i, ref, row0):
        a, b = local[i]
        a.wait()
        b.wait()
        t = lax.dot_general(eye, rem_in[i], (((1,), (1,)), ((), ())), preferred_element_type=F32)
        ref[pl.ds(row0, REM), :] = jnp.zeros((REM, MAIN), BF)
        ref[pl.ds(row0, REM), pl.ds(0, PIECE)] = t.astype(BF)

    n = 0
    zrow = pl.multiple_of(z * SLOT, 16)
    for o, (dxh, dy) in enumerate(OFFS):
        for kk in range(2):
            add_rem(n, stage.at[n], PIECE)
            cc = col(xh + dxh - 2 * xh * dxh, y + dy, kk)
            rr = row_flip if dxh else r
            send(remote(stage.at[n], irecv.at[c, pl.ds(zrow, SLOT), :], p1_send.at[n], p1_recv.at[o, k], rr, cc))
            n += 1
    for f in range(3):
        for q in range(4):
            add_rem(n, stage_full.at[f], q * SLOT + PIECE)
            n += 1
        send(remote(stage_full.at[f], irecv.at[c], full_send.at[f],
                    full_recv.at[0] if f == 0 else full_recv.at[1 + k], r if f == 0 else row_flip, full_c[f]))
    for q in range(4):
        add_rem(n, irecv.at[c], q * SLOT + PIECE)
        n += 1

    def table(b, carry):
        j = lax.broadcasted_iota(jnp.int32, (128, NPAD), 0)
        col_i = lax.broadcasted_iota(jnp.int32, (128, NPAD), 1) - 50 * b
        e1[pl.ds(pl.multiple_of(b * 128, 128), 128), :] = jnp.where((j < 50) & (col_i == j), 1.0, 0.0).astype(BF)
        e2[pl.ds(pl.multiple_of(b * 128, 128), 128), :] = jnp.where(
            (j >= 50) & (j < 100) & (col_i == j - 50), 1.0, 0.0).astype(BF)
        return carry
    lax.fori_loop(0, 16, table, 0)
    s_buf[pl.ds(TILE, NPAD - TILE), :] = jnp.zeros((NPAD - TILE, NPAD), BF)

    def src_col(o, kk):
        dxh, dy = OFFS[o]
        return col(xh + dxh - 2 * xh * dxh, y + 4 - dy, kk)

    up, down = ((z + 1) % 4) * 2 + xl, ((z + 3) % 4) * 2 + xl
    zrows = [pl.multiple_of(((z + d) % 4) * SLOT, 16) for d in range(4)]

    def i_slot(o, kk, d):
        return irecv.at[src_col(o, kk), pl.ds(zrows[d], SLOT), :]

    def share(o):
        for kk in range(2):
            ref = i_slot(o, kk, 0)
            remote(ref, ref, p1_send.at[0], p1_recv.at[o, kk], r, c).wait_recv()
            send(remote(ref, ref, z_send.at[o, kk, 0], z_recv.at[o, kk, 0], up, c))
            send(remote(ref, ref, z_send.at[o, kk, 1], z_recv.at[o, kk, 1], down, c))

    def pass_on(o):
        for kk in range(2):
            lo, hi = i_slot(o, kk, 3), i_slot(o, kk, 1)
            first, second = ((lo, 0), (hi, 1)) if kk == 0 else ((hi, 1), (lo, 0))
            remote(first[0], first[0], z_send.at[o, kk, 0], z_recv.at[o, kk, first[1]], r, c).wait_recv()
            send(remote(first[0], first[0], z2_send.at[o, kk], z2_recv.at[o, kk], up if kk == 0 else down, c))
        for kk in range(2):
            lo, hi = i_slot(o, kk, 3), i_slot(o, kk, 1)
            second = (hi, 1) if kk == 0 else (lo, 0)
            remote(second[0], second[0], z_send.at[o, kk, 0], z_recv.at[o, kk, second[1]], r, c).wait_recv()

    def arrived(o):
        for kk in range(2):
            ref = i_slot(o, kk, 2)
            remote(ref, ref, z_send.at[o, kk, 0], z2_recv.at[o, kk], r, c).wait_recv()

    own1.wait()
    for d in range(1, 16):
        cc = (c + 16 - d) % 16
        remote(sendbuf.at[0], mid.at[:, cc], s1_send.at[d], s1_recv.at[d], r, c).wait_recv()
    for d in range(1, 8):
        rr = (r + d) % 8
        send(remote(mid.at[rr], fin.at[pl.ds(pl.multiple_of(r * 16, 16), 16)], s2_send.at[d], s2_recv.at[d], rr, c))
    own2 = pltpu.make_async_copy(mid.at[r], fin.at[pl.ds(pl.multiple_of(r * 16, 16), 16)], s2_send.at[0])
    own2.start()

    share(0)
    share(1)

    own2.wait()
    for d in range(1, 8):
        rr = (r + 8 - d) % 8
        remote(mid.at[0], fin.at[pl.ds(pl.multiple_of(rr * 16, 16), 16)], s2_send.at[d], s2_recv.at[d], r, c).wait_recv()

    def put(a, carry):
        for b in range(16):
            x_buf[pl.ds(pl.multiple_of(32 * a, 32), 32), pl.ds(128 * b, 128)] = fin[owner[16 * a + b]]
        return carry
    lax.fori_loop(0, 8, put, 0)
    m_i = lax.broadcasted_iota(jnp.int32, (KB, 256), 0)
    n_i = lax.broadcasted_iota(jnp.int32, (KB, 256), 1)
    blk = (m_i * 1311) >> 16
    inner = m_i - 50 * blk
    f1 = jnp.where((inner < 32) & (n_i == 32 * blk + inner), 1.0, 0.0).astype(BF)
    f2 = jnp.where((inner >= 32) & (n_i == 32 * blk + inner - 32), 1.0, 0.0).astype(BF)
    own_half = s_buf.at[pl.ds(pl.multiple_of(k * KB, 16), KB), :]
    mate_half = s_buf.at[pl.ds(pl.multiple_of((1 - k) * KB, 16), KB), :]
    def place(i, carry):
        at = pl.ds(pl.multiple_of(i * 128, 128), 128)
        y1 = jnp.dot(x_buf[...], e1[:, at], preferred_element_type=F32).astype(BF)
        y2 = jnp.dot(x_buf[...], e2[:, at], preferred_element_type=F32).astype(BF)
        part = jnp.dot(f1, y1, preferred_element_type=F32) + jnp.dot(f2, y2, preferred_element_type=F32)
        s_buf[pl.ds(pl.multiple_of(k * KB, 16), KB), at] = part.astype(BF)
        return carry
    lax.fori_loop(0, 7, place, 0)
    send(remote(own_half, own_half, ex_send.at[0], ex_recv.at[0], r, mate))
    share(2)
    remote(mate_half, mate_half, ex_send.at[0], ex_recv.at[0], r, c).wait_recv()
    def turn(i, carry):
        at = pl.ds(pl.multiple_of(i * 128, 128), 128)
        st_buf[:, at] = s_buf[at, pl.ds(pl.multiple_of(k * MAIN, 128), 512)].T
        return carry
    lax.fori_loop(0, 7, turn, 0)

    def choose(i, carry):
        row0 = pl.multiple_of(i * 80, 16)
        straight = s_buf[pl.ds(pl.multiple_of(k * KB + row0, 16), 80), :]
        flipped = st_buf[pl.ds(pl.multiple_of(16 * k + row0, 16), 80), :]
        g_k = lax.broadcasted_iota(jnp.int32, (80, NPAD), 0) + (c * KB + row0)
        g_n = lax.broadcasted_iota(jnp.int32, (80, NPAD), 1) + r * TILE
        tile = jnp.where(g_k <= g_n, straight.astype(F32), flipped.astype(F32))
        tile = jnp.where(mask[pl.ds(row0, 80), :] > 0, tile, 0.0)
        arecv[c, pl.ds(row0, 80), :] = tile.astype(BF)
        return carry
    lax.fori_loop(0, 5, choose, 0)

    yup, ydown = col(xh, y + 1, k), col(xh, y + 3, k)

    def a_send_to(cc, i, j, dest):
        send(remote(arecv.at[cc], arecv.at[cc], a_send.at[i], a_recv.at[j], r, dest))

    def a_wait(cc, j):
        remote(arecv.at[cc], arecv.at[cc], a_send.at[0], a_recv.at[j], r, c).wait_recv()

    def xy(dxh, dy, kk):
        return col(xh + dxh - 2 * xh * dxh, y + dy + 4, kk)

    a_send_to(c, 0, 1, yup)
    a_send_to(c, 1, 2, ydown)
    a_send_to(c, 2, 0, cross_c)
    a_send_to(c, 3, 8, mate)

    def product(cc, first=False):
        def cut(n0, nw):
            part = jnp.dot(irecv[cc], arecv[cc, pl.ds(0, MAIN), pl.ds(n0, nw)], preferred_element_type=F32)
            if first:
                acc[:, pl.ds(n0, nw)] = part
            else:
                acc[:, pl.ds(n0, nw)] += part

        def step(i, carry):
            cut(pl.multiple_of(i * 256, 256), 256)
            return carry
        lax.fori_loop(0, 3, step, 0)
        cut(768, 128)

    product(c, True)
    share(3)
    share(4)
    share(5)
    a_wait(cross_c, 0)
    a_send_to(cross_c, 4, 3, yup)
    a_send_to(cross_c, 5, 4, ydown)
    a_send_to(cross_c, 6, 9, mate)
    pass_on(0)
    pass_on(1)
    a_wait(xy(0, -1, k), 1)
    a_send_to(xy(0, -1, k), 7, 5, yup)
    a_send_to(xy(0, -1, k), 8, 10, mate)
    a_wait(xy(0, 1, k), 2)
    a_send_to(xy(0, 1, k), 9, 11, mate)
    full = irecv.at[mate]
    remote(full, full, full_send.at[0], full_recv.at[0], r, c).wait_recv()
    a_wait(mate, 8)
    product(mate)
    for kk in range(2):
        full = irecv.at[xy(1, 0, kk)]
        remote(full, full, full_send.at[0], full_recv.at[1 + kk], r, c).wait_recv()
    product(cross_c)
    a_wait(xy(1, 0, 1 - k), 9)
    product(xy(1, 0, 1 - k))
    pass_on(2)
    pass_on(3)
    a_wait(xy(1, 1, k), 4)
    a_send_to(xy(1, 1, k), 10, 6, ydown)
    a_send_to(xy(1, 1, k), 11, 12, mate)
    a_wait(xy(1, -1, k), 3)
    a_send_to(xy(1, -1, k), 12, 13, mate)
    pass_on(4)
    pass_on(5)
    arrived(0)
    arrived(1)
    for dy, j in ((-1, 10), (1, 11)):
        product(xy(0, dy, k))
        a_wait(xy(0, dy, 1 - k), j)
        product(xy(0, dy, 1 - k))
    a_wait(xy(0, 2, k), 5)
    a_send_to(xy(0, 2, k), 13, 14, mate)
    arrived(2)
    arrived(3)
    for dy, j in ((1, 12), (-1, 13)):
        product(xy(1, dy, k))
        a_wait(xy(1, dy, 1 - k), j)
        product(xy(1, dy, 1 - k))
    a_wait(xy(1, 2, k), 6)
    a_send_to(xy(1, 2, k), 14, 15, mate)
    arrived(4)
    arrived(5)
    product(xy(0, 2, k))
    product(xy(1, 2, k))
    a_wait(xy(0, 2, 1 - k), 14)
    product(xy(0, 2, 1 - k))
    a_wait(xy(1, 2, 1 - k), 15)
    product(xy(1, 2, 1 - k))

    for cc in range(16):
        arem[pl.ds(16 * cc, 16), :] = arecv[cc, pl.ds(MAIN, REM), :]
        for q in range(4):
            l_buf[q, pl.ds(16 * cc, 16), :] = irecv[cc, pl.ds(q * SLOT + PIECE, REM), pl.ds(0, 256)]
    for q, (skip, row0) in enumerate(((0, 0), (16, 208), (16, 400), (0, 592))):
        part = lax.dot_general(l_buf[q], arem[...], (((0,), (0,)), ((), ())), preferred_element_type=F32)
        rows = PIECE - skip
        total = acc[pl.ds(q * SLOT + skip, rows), pl.ds(0, TILE)] + part[skip:PIECE, :TILE]
        out[pl.ds(row0, rows), :] = total.astype(BF)

    for cp in sends:
        cp.wait_send()


def slot_table(owner_map, me):
    index = jnp.arange(128, dtype=jnp.int32)
    mine = jnp.sum(jnp.where(owner_map == me, index, 0))
    a, b = mine // 16, mine % 16
    rr, cc = index // 16, index % 16
    lo, hi, h = jnp.minimum(rr, cc // 2), jnp.maximum(rr, cc // 2), cc % 2
    e0 = (a > b).astype(jnp.int32)
    e1 = (a + 8 > b).astype(jnp.int32)
    down = 2 * lo + h
    before = 8 * down - (lo * (lo - 1) + lo * (e0 + e1) + h * (lo + e0))
    first = lo + jnp.where(h == 1, e1, e0)
    return jnp.clip(before + hi - first, 0, 71)


def body(integrals, packed_store, pair_sector, owner_map):
    r = lax.axis_index("row")
    c = lax.axis_index("col")
    slots = slot_table(owner_map, r * 16 + c)
    pad = jnp.zeros((72, 14, 50), BF)
    low = jnp.concatenate([packed_store[:, 32:, :], pad], axis=1)
    packed = jnp.concatenate([packed_store[:, :32, :], low, jnp.zeros((72, 32, 28), BF)], axis=2)
    rows = lax.dynamic_slice_in_dim(pair_sector, c * KB, KB, 0)
    cols = lax.dynamic_slice_in_dim(pair_sector, r * TILE, TILE, 0)
    cols = jnp.pad(cols, (0, NPAD - TILE), constant_values=-1)
    mask = (rows[:, None] == cols[None, :]).astype(F32)
    dma = pltpu.SemaphoreType.DMA
    vm = lambda *s: pltpu.VMEM(s, BF)
    return pl.pallas_call(
        kernel,
        out_shape=jax.ShapeDtypeStruct((TILE, TILE), BF),
        in_specs=[pl.BlockSpec(memory_space=pltpu.SMEM)] * 2 + [pl.BlockSpec(memory_space=pl.ANY)]
        + [pl.BlockSpec(memory_space=pltpu.VMEM)] * 2,
        out_specs=pl.BlockSpec(memory_space=pltpu.VMEM),
        scratch_shapes=[
            vm(16, 8, 32, 128), vm(8, 16, 32, 128), vm(128, 32, 128),
            vm(28, PIECE, REM), vm(12, SLOT, MAIN), vm(3, ROWS, MAIN), vm(16, ROWS, MAIN), vm(16, KB, NPAD),
            vm(256, 2048), vm(2048, NPAD), vm(2048, NPAD), vm(NPAD, NPAD), vm(512, NPAD),
            pltpu.VMEM((ROWS, NPAD), F32), vm(4, 256, 256), vm(256, NPAD),
            dma((28,)), dma((28,)), dma((16,)), dma((16,)), dma((8,)), dma((8,)),
            dma((12,)), dma((6, 2)), dma((3,)), dma((3,)),
            dma((6, 2, 2)), dma((6, 2, 2)), dma((6, 2)), dma((6, 2)), dma((1,)), dma((1,)),
            dma((15,)), dma((16,)),
        ],
        compiler_params=pltpu.CompilerParams(has_side_effects=True, vmem_limit_bytes=60 * 2**20),
        cost_estimate=pl.CostEstimate(flops=2 * 800 * 800 * 6400, bytes_accessed=20_000_000, transcendentals=0),
    )(slots, owner_map, integrals, packed, mask)


def solution(mesh):
    in_specs = (P(None, "col"), P(("row", "col"), None, None), P(), P())
    return jax.shard_map(body, mesh=mesh, in_specs=in_specs, out_specs=P("col", "row"), check_vma=False)
```

```python
import functools

import jax
import jax.numpy as jnp
from jax import lax
from jax.experimental import pallas as pl
from jax.experimental.pallas import tpu as pltpu
from jax.sharding import PartitionSpec as P

MESH = pl.DeviceIdType.MESH
BF = jnp.bfloat16
F32 = jnp.float32

TILE = 800
KB = 400
MAIN = 384
REM = 16
PIECE = 208
SLOT = PIECE + REM
ROWS = 4 * SLOT
NPAD = 896
SHIFTS = (1, 3, 2)
OFFS = [(dxh, dy) for dxh in range(2) for dy in SHIFTS]
LATE_XL = ()
P1_EARLY = True
ORDER = ('P0', 'P1', 'P2', 'P3', 'P4', 'P5', 'X0', 'U00', 'E1', 'X1', 'X2', 'X3', 'X4', 'X5', 'U10', 'U20', 'E2', 'U30', 'U40', 'U50', 'M0', 'U01', 'L', 'H', 'U11', 'U21', 'U31', 'U41', 'U51', 'C', 'M1', 'M2', 'G', 'M3', 'M4', 'Q', 'M6', 'J', 'M5', 'R', 'M7')


def piece_start(q):
    return 192 * q + 16 * (q // 3)


def kernel(slots, owner, integrals, packed, sector, out,
           sendbuf, fin, win, win_full, stage, stage_full, irecv, arecv,
           x_buf, e1, e2, s_buf, st_buf, acc, l_buf, arem, sec_rows,
           w_sem, wf_sem, s1_send, s1_recv, own_sem, p1_send, p1_recv, full_send, full_recv,
           z_send, z_recv, z2_send, z2_recv, xl_send, xl_recv, ex_send, ex_recv, a_send, a_recv):
    r = lax.axis_index("row")
    c = lax.axis_index("col")
    z, xl = r // 2, r % 2
    xh, y, k = c // 8, (c // 2) % 4, c % 2

    def col(xh_, y_, k_):
        return xh_ * 8 + (y_ % 4) * 2 + k_

    def remote(src, dst, ssem, rsem_, row_, col_):
        return pltpu.make_async_remote_copy(src_ref=src, dst_ref=dst, send_sem=ssem, recv_sem=rsem_,
                                            device_id=(row_, col_), device_id_type=MESH)

    sends = []

    def send(cp):
        cp.start()
        sends.append(cp)

    mate = c + 1 - 2 * k
    cross_c = c + 8 - 16 * xh
    row_flip = z * 2 + 1 - xl

    dx = (k + xl) % 2
    p_xh = (xh + dx) % 2
    p_row = z * 2 + (xl + dx) % 2
    p_cols = [col(p_xh, y + dy, kk) for dy in SHIFTS for kk in range(2)]
    full_c = [mate, col(1 - xh, y, 0), col(1 - xh, y, 1), c]

    def window(start, width):
        first = jnp.minimum(start // 128, (12800 - width) // 128) * 128
        return pl.multiple_of(first, 128), start - first

    win_off, win_cp = [], []
    for n in range(6):
        w0, off = window(p_cols[n] * TILE + piece_start(z), 384)
        cp = pltpu.make_async_copy(integrals.at[:, pl.ds(w0, 384)], win.at[n], w_sem.at[n])
        cp.start()
        win_off.append(off)
        win_cp.append(cp)
    full_off, full_cp = [], []
    for f in range(4):
        w0, off = window(full_c[f] * TILE, 896)
        cp = pltpu.make_async_copy(integrals.at[:, pl.ds(w0, 896)], win_full.at[f], wf_sem.at[f])
        cp.start()
        full_off.append(off)
        full_cp.append(cp)

    me = r * 16 + c

    def pick(n, carry):
        sendbuf[n] = packed[slots[n]]
        return carry
    lax.fori_loop(0, 128, pick, 0, unroll=8)

    def give(d, carry):
        to = (me + d) % 128
        remote(sendbuf.at[to], fin.at[me], s1_send, s1_recv, to // 16, to % 16).start()
        return carry
    lax.fori_loop(1, 128, give, 0)
    own1 = pltpu.make_async_copy(sendbuf.at[me], fin.at[me], own_sem)
    own1.start()

    def turn_piece(read, off, store):
        i = lax.broadcasted_iota(jnp.int32, (256, 384), 0)
        lane = lax.broadcasted_iota(jnp.int32, (256, 384), 1)
        pick_rows = jnp.where((i < PIECE) & (lane == i + off), 1.0, 0.0).astype(BF)
        dims = (((1,), (1,)), ((), ()))
        main = lax.dot_general(pick_rows[:PIECE], read(0, MAIN), dims, preferred_element_type=F32)
        rest = lax.dot_general(read(MAIN, REM), pick_rows, dims, preferred_element_type=F32)
        store(main.astype(BF), rest.astype(BF))

    def into(ref, row0):
        def store(main, rest):
            ref[pl.ds(row0, PIECE), :] = main
            ref[pl.ds(row0 + PIECE, REM), pl.ds(0, 256)] = rest
            ref[pl.ds(row0 + PIECE, REM), pl.ds(256, 128)] = jnp.zeros((REM, 128), BF)
        return store

    zrow = pl.multiple_of(z * SLOT, 16)

    def send_p1():
        for n in range(6):
            send(remote(stage.at[n], irecv.at[c, pl.ds(zrow, SLOT), :], p1_send.at[n],
                        p1_recv.at[dx * 3 + n // 2], p_row, p_cols[n]))

    for n in range(6):
        win_cp[n].wait()
        turn_piece(lambda k0, kn: win[n, pl.ds(k0, kn), :], win_off[n], into(stage.at[n], 0))
    if P1_EARLY:
        send_p1()

    def turn_full(f, ref):
        full_cp[f].wait()

        def one(q, carry):
            at = full_off[f] + piece_start(q)
            lane0 = jnp.minimum(at // 128, 4) * 128
            turn_piece(lambda k0, kn: win_full[f, pl.ds(k0, kn), pl.ds(pl.multiple_of(lane0, 128), 384)],
                       at - lane0, into(ref, pl.multiple_of(q * SLOT, 16)))
            return carry
        lax.fori_loop(0, 4, one, 0)

    for f in (1, 2, 0):
        turn_full(f, stage_full.at[f])
        send(remote(stage_full.at[f], irecv.at[c], full_send.at[f],
                    full_recv.at[0] if f == 0 else full_recv.at[1 + k], r if f == 0 else row_flip, full_c[f]))

    def table(b, carry):
        j = lax.broadcasted_iota(jnp.int32, (128, NPAD), 0)
        col_i = lax.broadcasted_iota(jnp.int32, (128, NPAD), 1) - 50 * b
        e1[pl.ds(pl.multiple_of(b * 128, 128), 128), :] = jnp.where((j < 50) & (col_i == j), 1.0, 0.0).astype(BF)
        e2[pl.ds(pl.multiple_of(b * 128, 128), 128), :] = jnp.where(
            (j >= 50) & (j < 100) & (col_i == j - 50), 1.0, 0.0).astype(BF)
        return carry
    lax.fori_loop(0, 16, table, 0)
    s_buf[pl.ds(TILE, NPAD - TILE), :] = jnp.zeros((NPAD - TILE, NPAD), BF)

    def src_col(o, half):
        dxh, dy = OFFS[o]
        core = xl if half == 0 else 1 - xl
        return col(xh + dxh - 2 * xh * dxh, y + 4 - dy, core)

    up, down = ((z + 1) % 4) * 2 + xl, ((z + 3) % 4) * 2 + xl
    zrows = [pl.multiple_of(((z + d) % 4) * SLOT, 16) for d in range(4)]

    def i_slot(o, half, d):
        return irecv.at[src_col(o, half), pl.ds(zrows[d], SLOT), :]

    def i_wait(ref, sem):
        remote(ref, ref, p1_send.at[0], sem, r, c).wait_recv()

    def to_xl(o, d):
        ref = i_slot(o, 0, d)
        send(remote(ref, ref, xl_send.at[o, d], xl_recv.at[o, d], row_flip, c))

    def both_ways(o, half):
        ref = i_slot(o, half, 0)
        send(remote(ref, ref, z_send.at[o, half, 0], z_recv.at[o, half, 0], up, c))
        send(remote(ref, ref, z_send.at[o, half, 1], z_recv.at[o, half, 1], down, c))

    def share(o):
        i_wait(i_slot(o, 0, 0), p1_recv.at[o])
        to_xl(o, 0)
        both_ways(o, 0)

    def share_xl(o):
        i_wait(i_slot(o, 1, 0), xl_recv.at[o, 0])
        if o not in LATE_XL:
            both_ways(o, 1)

    def one_end(o, half):
        d = 3 if half == 0 else 1
        ref = i_slot(o, half, d)
        i_wait(ref, z_recv.at[o, half, half])
        send(remote(ref, ref, z2_send.at[o, half], z2_recv.at[o, half], up if half == 0 else down, c))
        if o in LATE_XL:
            to_xl(o, d)

    def other_end(o, half):
        d = 1 if half == 0 else 3
        i_wait(i_slot(o, half, d), z_recv.at[o, half, 1 - half])
        if o in LATE_XL:
            to_xl(o, d)

    def far_end(o, half):
        i_wait(i_slot(o, half, 2), z2_recv.at[o, half])
        if o in LATE_XL:
            to_xl(o, 2)

    def rest_of(o):
        if o in LATE_XL:
            for d in (1, 3, 2):
                i_wait(i_slot(o, 1, d), xl_recv.at[o, d])
        else:
            other_end(o, 0)
            far_end(o, 0)
            other_end(o, 1)
            far_end(o, 1)

    if not P1_EARLY:
        send_p1()
    turn_full(3, irecv.at[c])

    def line(first, count):
        at = first // 128
        parts = [sector[pl.ds(jnp.minimum(at + i, 49), 1), :] for i in range(count)]
        flat = jnp.broadcast_to(jnp.concatenate(parts, axis=1), (8, 128 * count))
        return pltpu.roll(flat, 128 * count - (first - at * 128), axis=1)
    sec_cols = line(r * TILE, 8)[0:1, :NPAD]
    sec_rows[...] = jnp.broadcast_to(line(c * KB, 5)[0:1, :512], (128, 512)).astype(F32).T
    sec_cols = sec_cols.astype(F32)

    own_half = s_buf.at[pl.ds(pl.multiple_of(k * KB, 16), KB), :]
    mate_half = s_buf.at[pl.ds(pl.multiple_of((1 - k) * KB, 16), KB), :]

    def assemble():
        own1.wait()
        remote(sendbuf.at[pl.ds(0, 127)], fin.at[pl.ds(0, 127)], s1_send, s1_recv, r, c).wait_recv()

        def put(a, carry):
            for b in range(16):
                x_buf[pl.ds(pl.multiple_of(32 * a, 32), 32), pl.ds(128 * b, 128)] = fin[owner[16 * a + b]]
            return carry
        lax.fori_loop(0, 8, put, 0)
        m_i = lax.broadcasted_iota(jnp.int32, (KB, 256), 0)
        n_i = lax.broadcasted_iota(jnp.int32, (KB, 256), 1)
        blk = (m_i * 1311) >> 16
        inner = m_i - 50 * blk
        f1 = jnp.where((inner < 32) & (n_i == 32 * blk + inner), 1.0, 0.0).astype(BF)
        f2 = jnp.where((inner >= 32) & (n_i == 32 * blk + inner - 32), 1.0, 0.0).astype(BF)
        for n0, nw, k0, kw in ((0, 256, 0, 768), (256, 256, 640, 768), (512, 256, 1280, 768), (768, 128, 1920, 128)):
            x = x_buf[:, pl.ds(k0, kw)]
            y1 = jnp.dot(x, e1[pl.ds(k0, kw), pl.ds(n0, nw)], preferred_element_type=F32).astype(BF)
            y2 = jnp.dot(x, e2[pl.ds(k0, kw), pl.ds(n0, nw)], preferred_element_type=F32).astype(BF)
            part = jnp.dot(f1, y1, preferred_element_type=F32) + jnp.dot(f2, y2, preferred_element_type=F32)
            s_buf[pl.ds(pl.multiple_of(k * KB, 16), KB), pl.ds(n0, nw)] = part.astype(BF)
        send(remote(own_half, own_half, ex_send.at[0], ex_recv.at[0], r, mate))

    yup, ydown = col(xh, y + 1, k), col(xh, y + 3, k)

    def a_send_to(cc, i, j, dest):
        send(remote(arecv.at[cc], arecv.at[cc], a_send.at[i], a_recv.at[j], r, dest))

    def a_wait(cc, j):
        remote(arecv.at[cc], arecv.at[cc], a_send.at[0], a_recv.at[j], r, c).wait_recv()

    def xy(dxh, dy, kk):
        return col(xh + dxh - 2 * xh * dxh, y + dy + 4, kk)

    def complete():
        remote(mate_half, mate_half, ex_send.at[0], ex_recv.at[0], r, c).wait_recv()

        def turn(i, carry):
            at = pl.ds(pl.multiple_of(i * 128, 128), 128)
            st_buf[:, at] = s_buf[at, pl.ds(pl.multiple_of(k * MAIN, 128), 512)].T
            return carry
        lax.fori_loop(0, 7, turn, 0)

        def choose(i, carry):
            row0 = pl.multiple_of(i * 80, 16)
            straight = s_buf[pl.ds(pl.multiple_of(k * KB + row0, 16), 80), :]
            flipped = st_buf[pl.ds(pl.multiple_of(16 * k + row0, 16), 80), :]
            g_k = lax.broadcasted_iota(jnp.int32, (80, NPAD), 0) + (c * KB + row0)
            g_n = lax.broadcasted_iota(jnp.int32, (80, NPAD), 1) + r * TILE
            tile = jnp.where(g_k <= g_n, straight.astype(F32), flipped.astype(F32))
            tile = jnp.where(sec_rows[pl.ds(row0, 80), 0:1] == sec_cols, tile, 0.0)
            arecv[c, pl.ds(row0, 80), :] = tile.astype(BF)
            return carry
        lax.fori_loop(0, 5, choose, 0)
        a_send_to(c, 0, 1, yup)
        a_send_to(c, 1, 2, ydown)
        a_send_to(c, 2, 0, cross_c)
        a_send_to(c, 3, 8, mate)

    def from_x():
        a_wait(cross_c, 0)
        a_send_to(cross_c, 4, 3, yup)
        a_send_to(cross_c, 5, 4, ydown)
        a_send_to(cross_c, 6, 9, mate)

    def from_y(dxh, dy, j, on, to_mate):
        cc = xy(dxh, dy, k)
        a_wait(cc, j)
        if on is not None:
            a_send_to(cc, *on)
        a_send_to(cc, *to_mate, mate)

    def product(dxh, dy, first):
        c0, c1 = xy(dxh, dy, 0), xy(dxh, dy, 1)

        def cut(n0, nw):
            at = pl.ds(n0, nw)
            left = jnp.concatenate([irecv[c0], irecv[c1]], axis=1)
            right = jnp.concatenate([arecv[c0, pl.ds(0, MAIN), at], arecv[c1, pl.ds(0, MAIN), at]], axis=0)
            part = jnp.dot(left, right, preferred_element_type=F32)
            if first:
                acc[:, at] = part
            else:
                acc[:, at] += part

        def step(i, carry):
            cut(pl.multiple_of(i * 256, 256), 256)
            return carry
        lax.fori_loop(0, 3, step, 0)
        cut(768, 128)

    def whole(cc, sem):
        ref = irecv.at[cc]
        remote(ref, ref, full_send.at[0], full_recv.at[sem], r, c).wait_recv()

    def multiply(i, first):
        dxh, dy, j = ((0, 0, 8), (1, 0, 9), (0, -1, 10), (0, 1, 11), (1, 1, 12), (1, -1, 13), (0, 2, 14), (1, 2, 15))[i]
        if i == 0:
            whole(mate, 0)
        elif i == 1:
            whole(xy(1, 0, 0), 1)
            whole(xy(1, 0, 1), 2)
        else:
            rest_of(dxh * 3 + {-1: 0, 1: 1, 2: 2}[dy])
        a_wait(xy(dxh, dy, 1 - k), j)
        product(dxh, dy, first)

    steps = {"E1": assemble, "E2": complete, "C": from_x}
    for o in range(6):
        steps["P%d" % o] = functools.partial(share, o)
        steps["X%d" % o] = functools.partial(share_xl, o)
        for half in range(2):
            steps["U%d%d" % (o, half)] = functools.partial(one_end, o, half)
            steps["V%d%d" % (o, half)] = functools.partial(other_end, o, half)
            steps["W%d%d" % (o, half)] = functools.partial(far_end, o, half)
    steps["L"] = functools.partial(from_y, 0, -1, 1, (7, 5, yup), (8, 10))
    steps["H"] = functools.partial(from_y, 0, 1, 2, None, (9, 11))
    steps["G"] = functools.partial(from_y, 1, 1, 4, (10, 6, ydown), (11, 12))
    steps["J"] = functools.partial(from_y, 1, -1, 3, None, (12, 13))
    steps["Q"] = functools.partial(from_y, 0, 2, 5, None, (13, 14))
    steps["R"] = functools.partial(from_y, 1, 2, 6, None, (14, 15))
    first = True
    for name in ORDER:
        if name[0] == "M":
            multiply(int(name[1:]), first)
            first = False
        else:
            steps[name]()

    for cc in range(16):
        arem[pl.ds(16 * cc, 16), :] = arecv[cc, pl.ds(MAIN, REM), :]
        for q in range(4):
            l_buf[q, pl.ds(16 * cc, 16), :] = irecv[cc, pl.ds(q * SLOT + PIECE, REM), pl.ds(0, 256)]
    for q, (skip, row0) in enumerate(((0, 0), (16, 208), (16, 400), (0, 592))):
        part = lax.dot_general(l_buf[q], arem[...], (((0,), (0,)), ((), ())), preferred_element_type=F32)
        rows = PIECE - skip
        total = acc[pl.ds(q * SLOT + skip, rows), pl.ds(0, TILE)] + part[skip:PIECE, :TILE]
        out[pl.ds(row0, rows), :] = total.astype(BF)

    for cp in sends:
        cp.wait_send()
    remote(sendbuf.at[pl.ds(0, 127)], fin.at[pl.ds(0, 127)], s1_send, s1_recv, r, c).wait_send()


def slot_table(owner_map, me):
    index = jnp.arange(128, dtype=jnp.int32)
    mine = jnp.sum(jnp.where(owner_map == me, index, 0))
    a, b = mine // 16, mine % 16
    rr, cc = index // 16, index % 16
    lo, hi, h = jnp.minimum(rr, cc // 2), jnp.maximum(rr, cc // 2), cc % 2
    e0 = (a > b).astype(jnp.int32)
    e1 = (a + 8 > b).astype(jnp.int32)
    down = 2 * lo + h
    before = 8 * down - (lo * (lo - 1) + lo * (e0 + e1) + h * (lo + e0))
    first = lo + jnp.where(h == 1, e1, e0)
    return jnp.clip(before + hi - first, 0, 71)


def body(integrals, packed_store, pair_sector, owner_map):
    r = lax.axis_index("row")
    c = lax.axis_index("col")
    slots = slot_table(owner_map, r * 16 + c)
    pad = jnp.zeros((72, 14, 50), BF)
    low = jnp.concatenate([packed_store[:, 32:, :], pad], axis=1)
    packed = jnp.concatenate([packed_store[:, :32, :], low, jnp.zeros((72, 32, 28), BF)], axis=2)
    dma = pltpu.SemaphoreType.DMA
    vm = lambda *s: pltpu.VMEM(s, BF)
    return pl.pallas_call(
        kernel,
        out_shape=jax.ShapeDtypeStruct((TILE, TILE), BF),
        in_specs=[pl.BlockSpec(memory_space=pltpu.SMEM)] * 2 + [pl.BlockSpec(memory_space=pl.ANY)]
        + [pl.BlockSpec(memory_space=pltpu.VMEM)] * 2,
        out_specs=pl.BlockSpec(memory_space=pltpu.VMEM),
        scratch_shapes=[
            vm(128, 32, 128), vm(128, 32, 128),
            vm(6, KB, 384), vm(4, KB, 896), vm(6, SLOT, MAIN), vm(3, ROWS, MAIN), vm(16, ROWS, MAIN), vm(16, KB, NPAD),
            vm(256, 2048), vm(2048, NPAD), vm(2048, NPAD), vm(NPAD, NPAD), vm(512, NPAD),
            pltpu.VMEM((ROWS, NPAD), F32), vm(4, 256, 256), vm(256, NPAD), pltpu.VMEM((512, 128), F32),
            dma((6,)), dma((4,)), dma, dma, dma,
            dma((6,)), dma((6,)), dma((3,)), dma((3,)),
            dma((6, 2, 2)), dma((6, 2, 2)), dma((6, 2)), dma((6, 2)), dma((6, 4)), dma((6, 4)), dma((1,)), dma((1,)),
            dma((15,)), dma((16,)),
        ],
        compiler_params=pltpu.CompilerParams(has_side_effects=True, vmem_limit_bytes=60 * 2**20),
        cost_estimate=pl.CostEstimate(flops=2 * 800 * 800 * 6400, bytes_accessed=20_000_000, transcendentals=0),
    )(slots, owner_map, integrals.T, packed, pair_sector.reshape(50, 128))


def solution(mesh):
    in_specs = (P(None, "col"), P(("row", "col"), None, None), P(), P())
    return jax.shard_map(body, mesh=mesh, in_specs=in_specs, out_specs=P("col", "row"), check_vma=False)
```

```python
import functools

import jax
import jax.numpy as jnp
from jax import lax
from jax.experimental import pallas as pl
from jax.experimental.pallas import tpu as pltpu
from jax.sharding import PartitionSpec as P

MESH = pl.DeviceIdType.MESH
BF = jnp.bfloat16
F32 = jnp.float32

TILE = 800
KB = 400
MAIN = 384
REM = 16
PIECE = 208
SLOT = PIECE + REM
ROWS = 4 * SLOT
NPAD = 896
NMAIN = 768
NROWS = KB + 32
WHOLE, LOW, HIGH = (0, NROWS), (0, 208), (208, 224)
CUTS_X = ((0, 144), (144, 144), (288, 144))
X_SEMS = ((2, 0), (17, 18), (18, 19))
SHIFTS = (1, 3, 2)
OFFS = [(dxh, dy) for dxh in range(2) for dy in SHIFTS]
LATE_XL = (4, 5)
EARLY = 2
ORDER = ('F0', 'P0', 'Y0', 'ZA0', 'P3', 'Y3', 'P1', 'S2', 'P4', 'Y1', 'ZA3', 'ZA1', 'ZA4', 'E1', 'X0', 'Y4', 'ZB0', 'E2', 'X3', 'P2', 'P5', 'X1', 'ZB3', 'ZB1', 'ZA5', 'ZA2', 'U00', 'F', 'U30', 'M00', 'X4', 'U10', 'M01', 'V40', 'U40', 'M02', 'M03', 'L', 'H', 'U01', 'U31', 'U11', 'V50', 'C', 'Y5', 'Y2', 'Q', 'U50', 'U20', 'M20', 'X5', 'X2', 'ZB2', 'M21', 'W40', 'M22', 'M23', 'M30', 'M31', 'M32', 'J', 'G', 'M33', 'U21', 'M50', 'M51', 'M52', 'M53', 'M40', 'M41', 'M42', 'W50', 'M43', 'M10', 'M11', 'M12', 'R', 'M13', 'M60', 'M61', 'M62', 'M63', 'M70', 'M71', 'M72', 'M73')


def piece_start(q):
    return 192 * q + 16 * (q // 3)


def kernel(slots, owner, integrals, packed, sector, out,
           sendbuf, fin, win, win_full, stage, stage_full, irecv, arecv,
           x_buf, e1, e2, s_buf, st_buf, acc, l_buf, arem, sec_rows, tail,
           w_sem, wf_sem, s1_send, s1_recv, own_sem, p1_send, p1_recv, full_send, full_recv,
           z_send, z_recv, z2_send, z2_recv, xl_send, xl_recv, ex_send, ex_recv, a_send, a_recv):
    r = lax.axis_index("row")
    c = lax.axis_index("col")
    z, xl = r // 2, r % 2
    xh, y, k = c // 8, (c // 2) % 4, c % 2

    def col(xh_, y_, k_):
        return xh_ * 8 + (y_ % 4) * 2 + k_

    def remote(src, dst, ssem, rsem_, row_, col_):
        return pltpu.make_async_remote_copy(src_ref=src, dst_ref=dst, send_sem=ssem, recv_sem=rsem_,
                                            device_id=(row_, col_), device_id_type=MESH)

    sends = []

    def send(cp):
        cp.start()
        sends.append(cp)

    mate = c + 1 - 2 * k
    cross_c = c + 8 - 16 * xh
    row_flip = z * 2 + 1 - xl

    me = r * 16 + c
    barrier = pltpu.get_barrier_semaphore()

    def greet(dr, carry):
        for dc in range(16):
            pl.semaphore_signal(barrier, inc=1, device_id=((r + dr) % 8, (c + dc) % 16), device_id_type=MESH)
        return carry
    for dc in range(1, 16):
        pl.semaphore_signal(barrier, inc=1, device_id=(r, (c + dc) % 16), device_id_type=MESH)
    lax.fori_loop(1, 8, greet, 0)

    dx = (k + xl) % 2
    p_xh = (xh + dx) % 2
    p_row = z * 2 + (xl + dx) % 2
    p_cols = [col(p_xh, y + dy, kk) for dy in SHIFTS for kk in range(2)]
    full_c = [mate, col(1 - xh, y, 0), col(1 - xh, y, 1), c]

    def window(start, width):
        first = jnp.minimum(start // 128, (12800 - width) // 128) * 128
        return pl.multiple_of(first, 128), start - first

    win_off, win_cp = [], []
    for n in range(6):
        w0, off = window(p_cols[n] * TILE + piece_start(z), 384)
        cp = pltpu.make_async_copy(integrals.at[:, pl.ds(w0, 384)], win.at[n], w_sem.at[n])
        cp.start()
        win_off.append(off)
        win_cp.append(cp)
    full_off, full_cp = [], []
    for f in range(4):
        w0, off = window(full_c[f] * TILE, 896)
        cp = pltpu.make_async_copy(integrals.at[:, pl.ds(w0, 896)], win_full.at[f], wf_sem.at[f])
        cp.start()
        full_off.append(off)
        full_cp.append(cp)

    def pick(n, carry):
        sendbuf[n] = packed[slots[n]]
        return carry
    lax.fori_loop(0, 128, pick, 0, unroll=8)

    def turn_piece(read, off, store):
        i = lax.broadcasted_iota(jnp.int32, (256, 384), 0)
        lane = lax.broadcasted_iota(jnp.int32, (256, 384), 1)
        pick_rows = jnp.where((i < PIECE) & (lane == i + off), 1.0, 0.0).astype(BF)
        dims = (((1,), (1,)), ((), ()))
        main = lax.dot_general(pick_rows[:PIECE], read(0, MAIN), dims, preferred_element_type=F32)
        rest = lax.dot_general(read(MAIN, REM), pick_rows, dims, preferred_element_type=F32)
        store(main.astype(BF), rest.astype(BF))

    def into(ref, row0):
        def store(main, rest):
            ref[pl.ds(row0, PIECE), :] = main
            ref[pl.ds(row0 + PIECE, REM), pl.ds(0, 256)] = rest
            ref[pl.ds(row0 + PIECE, REM), pl.ds(256, 128)] = jnp.zeros((REM, 128), BF)
        return store

    zrow = pl.multiple_of(z * SLOT, 16)

    def send_p1(i):
        for n in (2 * i, 2 * i + 1):
            send(remote(stage.at[n], irecv.at[c, pl.ds(zrow, SLOT), :], p1_send.at[n], p1_recv.at[dx * 3 + i], p_row, p_cols[n]))

    def stage_p1(n):
        win_cp[n].wait()
        turn_piece(lambda k0, kn: win[n, pl.ds(k0, kn), :], win_off[n], into(stage.at[n], 0))

    for n in range(2 * EARLY):
        stage_p1(n)
    pl.semaphore_wait(barrier, 127)
    for i in range(EARLY):
        send_p1(i)

    def give(to_r, to_c):
        to = to_r * 16 + to_c
        remote(sendbuf.at[to], fin.at[me], s1_send, s1_recv, to_r, to_c).start()

    def give_row(d, carry):
        for dc in range(16):
            give((r + d) % 8, (c + dc) % 16)
        return carry
    for dc in range(1, 16):
        give(r, (c + dc) % 16)
    lax.fori_loop(1, 8, give_row, 0)
    own1 = pltpu.make_async_copy(sendbuf.at[me], fin.at[me], own_sem)
    own1.start()
    for n in range(2 * EARLY, 6):
        stage_p1(n)

    def turn_full(f, ref):
        full_cp[f].wait()

        def one(q, carry):
            at = full_off[f] + piece_start(q)
            lane0 = jnp.minimum(at // 128, 4) * 128
            turn_piece(lambda k0, kn: win_full[f, pl.ds(k0, kn), pl.ds(pl.multiple_of(lane0, 128), 384)],
                       at - lane0, into(ref, pl.multiple_of(q * SLOT, 16)))
            return carry
        lax.fori_loop(0, 4, one, 0)

    def send_full(f):
        send(remote(stage_full.at[f], irecv.at[c], full_send.at[f],
                    full_recv.at[0] if f == 0 else full_recv.at[1 + k], r if f == 0 else row_flip, full_c[f]))

    def send_fulls():
        send_full(1)
        send_full(2)

    def prepare():
        for f in range(3):
            turn_full(f, stage_full.at[f])
        send_full(0)
        turn_full(3, irecv.at[c])
        lax.fori_loop(0, 16, table, 0)

    def table(b, carry):
        j = lax.broadcasted_iota(jnp.int32, (128, NPAD), 0)
        col_i = lax.broadcasted_iota(jnp.int32, (128, NPAD), 1) - 50 * b
        e1[pl.ds(pl.multiple_of(b * 128, 128), 128), :] = jnp.where((j < 50) & (col_i == j), 1.0, 0.0).astype(BF)
        e2[pl.ds(pl.multiple_of(b * 128, 128), 128), :] = jnp.where(
            (j >= 50) & (j < 100) & (col_i == j - 50), 1.0, 0.0).astype(BF)
        return carry
    tail[pl.ds(KB, 112), :] = jnp.zeros((112, 128), F32)
    s_buf[pl.ds(TILE, NPAD - TILE), :] = jnp.zeros((NPAD - TILE, NPAD), BF)

    def src_col(o, half):
        dxh, dy = OFFS[o]
        core = xl if half == 0 else 1 - xl
        return col(xh + dxh - 2 * xh * dxh, y + 4 - dy, core)

    up, down = ((z + 1) % 4) * 2 + xl, ((z + 3) % 4) * 2 + xl
    zrows = [pl.multiple_of(((z + d) % 4) * SLOT, 16) for d in range(4)]

    def i_slot(o, half, d):
        return irecv.at[src_col(o, half), pl.ds(zrows[d], SLOT), :]

    def i_wait(ref, sem):
        remote(ref, ref, p1_send.at[0], sem, r, c).wait_recv()

    def to_xl(o, d):
        ref = i_slot(o, 0, d)
        send(remote(ref, ref, xl_send.at[o, d], xl_recv.at[o, d], row_flip, c))

    def both_ways(o, half):
        ref = i_slot(o, half, 0)
        send(remote(ref, ref, z_send.at[o, half, 0], z_recv.at[o, half, 0], up, c))
        send(remote(ref, ref, z_send.at[o, half, 1], z_recv.at[o, half, 1], down, c))

    def shared(o):
        i_wait(i_slot(o, 0, 0), p1_recv.at[o])

    def shared_xl(o):
        i_wait(i_slot(o, 1, 0), xl_recv.at[o, 0])

    def one_end(o, half):
        d = 3 if half == 0 else 1
        ref = i_slot(o, half, d)
        i_wait(ref, z_recv.at[o, half, half])
        send(remote(ref, ref, z2_send.at[o, half], z2_recv.at[o, half], up if half == 0 else down, c))
        if o in LATE_XL:
            to_xl(o, d)

    def other_end(o, half):
        d = 1 if half == 0 else 3
        i_wait(i_slot(o, half, d), z_recv.at[o, half, 1 - half])
        if o in LATE_XL:
            to_xl(o, d)

    def far_end(o, half):
        i_wait(i_slot(o, half, 2), z2_recv.at[o, half])
        if o in LATE_XL:
            to_xl(o, 2)

    def rest_of(o):
        if o in LATE_XL:
            for d in (1, 3, 2):
                i_wait(i_slot(o, 1, d), xl_recv.at[o, d])
        else:
            other_end(o, 0)
            far_end(o, 0)
            other_end(o, 1)
            far_end(o, 1)

    def line(first, count):
        at = first // 128
        parts = [sector[pl.ds(jnp.minimum(at + i, 49), 1), :] for i in range(count)]
        flat = jnp.broadcast_to(jnp.concatenate(parts, axis=1), (8, 128 * count))
        return pltpu.roll(flat, 128 * count - (first - at * 128), axis=1)
    sec_cols = line(r * TILE, 8)[0:1, :NPAD]
    sec_rows[...] = jnp.broadcast_to(line(c * KB, 5)[0:1, :512], (128, 512)).astype(F32).T
    sec_cols = sec_cols.astype(F32)

    own_half = s_buf.at[pl.ds(pl.multiple_of(k * KB, 16), KB), :]
    mate_half = s_buf.at[pl.ds(pl.multiple_of((1 - k) * KB, 16), KB), :]

    def assemble():
        own1.wait()
        remote(sendbuf.at[pl.ds(0, 127)], fin.at[pl.ds(0, 127)], s1_send, s1_recv, r, c).wait_recv()

        def put(a, carry):
            for b in range(16):
                x_buf[pl.ds(pl.multiple_of(32 * a, 32), 32), pl.ds(128 * b, 128)] = fin[owner[16 * a + b]]
            return carry
        lax.fori_loop(0, 8, put, 0)
        m_i = lax.broadcasted_iota(jnp.int32, (KB, 256), 0)
        n_i = lax.broadcasted_iota(jnp.int32, (KB, 256), 1)
        blk = (m_i * 1311) >> 16
        inner = m_i - 50 * blk
        f1 = jnp.where((inner < 32) & (n_i == 32 * blk + inner), 1.0, 0.0).astype(BF)
        f2 = jnp.where((inner >= 32) & (n_i == 32 * blk + inner - 32), 1.0, 0.0).astype(BF)
        for n0, nw, k0, kw in ((0, 256, 0, 768), (256, 256, 640, 768), (512, 256, 1280, 768), (768, 128, 1920, 128)):
            x = x_buf[:, pl.ds(k0, kw)]
            y1 = jnp.dot(x, e1[pl.ds(k0, kw), pl.ds(n0, nw)], preferred_element_type=F32).astype(BF)
            y2 = jnp.dot(x, e2[pl.ds(k0, kw), pl.ds(n0, nw)], preferred_element_type=F32).astype(BF)
            part = jnp.dot(f1, y1, preferred_element_type=F32) + jnp.dot(f2, y2, preferred_element_type=F32)
            s_buf[pl.ds(pl.multiple_of(k * KB, 16), KB), pl.ds(n0, nw)] = part.astype(BF)
        send(remote(own_half, own_half, ex_send.at[0], ex_recv.at[0], r, mate))

    yup, ydown = col(xh, y + 1, k), col(xh, y + 3, k)

    def a_rows(cc, rows):
        return arecv.at[cc, pl.ds(rows[0], rows[1]), :]

    def a_send_to(cc, i, j, dest, rows=WHOLE):
        ref = a_rows(cc, rows)
        send(remote(ref, ref, a_send.at[i], a_recv.at[j], r, dest))

    def a_wait(cc, j, rows=WHOLE):
        ref = a_rows(cc, rows)
        remote(ref, ref, a_send.at[0], a_recv.at[j], r, c).wait_recv()

    def xy(dxh, dy, kk):
        return col(xh + dxh - 2 * xh * dxh, y + dy + 4, kk)

    def complete():
        remote(mate_half, mate_half, ex_send.at[0], ex_recv.at[0], r, c).wait_recv()

        def turn(i, carry):
            at = pl.ds(pl.multiple_of(i * 128, 128), 128)
            st_buf[:, at] = s_buf[at, pl.ds(pl.multiple_of(k * MAIN, 128), 512)].T
            return carry
        lax.fori_loop(0, 7, turn, 0)

        def choose(i, carry):
            row0 = pl.multiple_of(i * 80, 16)
            straight = s_buf[pl.ds(pl.multiple_of(k * KB + row0, 16), 80), :]
            flipped = st_buf[pl.ds(pl.multiple_of(16 * k + row0, 16), 80), :]
            g_k = lax.broadcasted_iota(jnp.int32, (80, NPAD), 0) + (c * KB + row0)
            g_n = lax.broadcasted_iota(jnp.int32, (80, NPAD), 1) + r * TILE
            tile = jnp.where(g_k <= g_n, straight.astype(F32), flipped.astype(F32))
            tile = jnp.where(sec_rows[pl.ds(row0, 80), 0:1] == sec_cols, tile, 0.0)
            arecv[c, pl.ds(row0, 80), :] = tile[:, :NMAIN].astype(BF)
            tail[pl.ds(row0, 80), :] = tile[:, NMAIN:]
            return carry
        lax.fori_loop(0, 5, choose, 0)
        arecv[c, pl.ds(KB, 32), pl.ds(0, 512)] = tail[...].T[:32].astype(BF)
        arecv[c, pl.ds(KB, 32), pl.ds(512, 256)] = jnp.zeros((32, 256), BF)
        arecv[c, pl.ds(KB, 16), pl.ds(512, 128)] = tail[pl.ds(MAIN, 16), :].astype(BF)
        for i, rows in enumerate(CUTS_X):
            a_send_to(c, X_SEMS[i][0], X_SEMS[i][1], cross_c, rows=rows)
        a_send_to(c, 0, 1, yup)
        a_send_to(c, 1, 2, ydown)
        a_send_to(c, 3, 8, mate)

    def from_x():
        for i, rows in enumerate(CUTS_X):
            a_wait(cross_c, X_SEMS[i][1], rows)
        a_send_to(cross_c, 4, 3, yup)
        a_send_to(cross_c, 5, 4, ydown)
        a_send_to(cross_c, 6, 9, mate)

    def from_y(dxh, dy, j, on, to_mate):
        cc = xy(dxh, dy, k)
        a_wait(cc, j)
        i, j2, dest, rows = on
        a_send_to(cc, i, j2, dest, rows=rows)
        a_send_to(cc, *to_mate, mate)

    def from_y2(dxh, low, high, to_mate):
        cc = xy(dxh, 2, k)
        a_wait(cc, low, LOW)
        a_wait(cc, high, HIGH)
        a_send_to(cc, *to_mate, mate)

    def product(dxh, dy, n, first):
        c0, c1 = xy(dxh, dy, 0), xy(dxh, dy, 1)

        def add(at, part):
            if first:
                acc[:, at] = part
            else:
                acc[:, at] += part

        left = jnp.concatenate([irecv[c0], irecv[c1]], axis=1)
        if n < 3:
            at = pl.ds(n * 256, 256)
            right = jnp.concatenate([arecv[c0, pl.ds(0, MAIN), at], arecv[c1, pl.ds(0, MAIN), at]], axis=0)
            add(at, jnp.dot(left, right, preferred_element_type=F32))
        else:
            side = pl.ds(KB, 32)
            right = jnp.concatenate([arecv[c0, side, pl.ds(0, MAIN)], arecv[c1, side, pl.ds(0, MAIN)]], axis=1)
            add(pl.ds(NMAIN, 32), lax.dot_general(left, right, (((1,), (1,)), ((), ())), preferred_element_type=F32))

    def whole(cc, sem):
        ref = irecv.at[cc]
        remote(ref, ref, full_send.at[0], full_recv.at[sem], r, c).wait_recv()

    def multiply(i, n, first):
        dxh, dy, j = ((0, 0, 8), (1, 0, 9), (0, -1, 10), (0, 1, 11), (1, 1, 12), (1, -1, 13), (0, 2, 14), (1, 2, 15))[i]
        if n > 0:
            product(dxh, dy, n, first)
            return
        if i == 0:
            whole(mate, 0)
        elif i == 1:
            whole(xy(1, 0, 0), 1)
            whole(xy(1, 0, 1), 2)
        else:
            rest_of(dxh * 3 + {-1: 0, 1: 1, 2: 2}[dy])
        a_wait(xy(dxh, dy, 1 - k), j)
        product(dxh, dy, n, first)

    steps = {"F": send_fulls, "F0": prepare, "E1": assemble, "E2": complete, "C": from_x}
    for i in range(3):
        steps["S%d" % i] = functools.partial(send_p1, i)
    for o in range(6):
        steps["P%d" % o] = functools.partial(shared, o)
        steps["X%d" % o] = functools.partial(shared_xl, o)
        steps["Y%d" % o] = functools.partial(to_xl, o, 0)
        steps["ZA%d" % o] = functools.partial(both_ways, o, 0)
        steps["ZB%d" % o] = functools.partial(both_ways, o, 1)
        for half in range(2):
            steps["U%d%d" % (o, half)] = functools.partial(one_end, o, half)
            steps["V%d%d" % (o, half)] = functools.partial(other_end, o, half)
            steps["W%d%d" % (o, half)] = functools.partial(far_end, o, half)
    steps["L"] = functools.partial(from_y, 0, -1, 1, (7, 5, yup, LOW), (8, 10))
    steps["H"] = functools.partial(from_y, 0, 1, 2, (15, 16, ydown, HIGH), (9, 11))
    steps["G"] = functools.partial(from_y, 1, 1, 4, (10, 6, ydown, HIGH), (11, 12))
    steps["J"] = functools.partial(from_y, 1, -1, 3, (16, 17, yup, LOW), (12, 13))
    steps["Q"] = functools.partial(from_y2, 0, 5, 16, (13, 14))
    steps["R"] = functools.partial(from_y2, 1, 17, 6, (14, 15))
    for name in ORDER:
        if name[0] == "M":
            multiply(int(name[1]), int(name[2]), name[1] == "0")
        else:
            steps[name]()

    for cc in range(16):
        arem[pl.ds(16 * cc, 16), pl.ds(0, NMAIN)] = arecv[cc, pl.ds(MAIN, REM), :]
        arem[pl.ds(16 * cc, 16), pl.ds(NMAIN, 128)] = arecv[cc, pl.ds(KB, 16), pl.ds(512, 128)]
        for q in range(4):
            l_buf[q, pl.ds(16 * cc, 16), :] = irecv[cc, pl.ds(q * SLOT + PIECE, REM), pl.ds(0, 256)]
    for q, (skip, row0) in enumerate(((0, 0), (16, 208), (16, 400), (0, 592))):
        part = lax.dot_general(l_buf[q], arem[...], (((0,), (0,)), ((), ())), preferred_element_type=F32)
        rows = PIECE - skip
        total = acc[pl.ds(q * SLOT + skip, rows), pl.ds(0, TILE)] + part[skip:PIECE, :TILE]
        out[pl.ds(row0, rows), :] = total.astype(BF)

    for cp in sends:
        cp.wait_send()
    remote(sendbuf.at[pl.ds(0, 127)], fin.at[pl.ds(0, 127)], s1_send, s1_recv, r, c).wait_send()


def slot_table(owner_map, me):
    index = jnp.arange(128, dtype=jnp.int32)
    mine = jnp.sum(jnp.where(owner_map == me, index, 0))
    a, b = mine // 16, mine % 16
    rr, cc = index // 16, index % 16
    lo, hi, h = jnp.minimum(rr, cc // 2), jnp.maximum(rr, cc // 2), cc % 2
    e0 = (a > b).astype(jnp.int32)
    e1 = (a + 8 > b).astype(jnp.int32)
    down = 2 * lo + h
    before = 8 * down - (lo * (lo - 1) + lo * (e0 + e1) + h * (lo + e0))
    first = lo + jnp.where(h == 1, e1, e0)
    return jnp.clip(before + hi - first, 0, 71)


def body(integrals, packed_store, pair_sector, owner_map):
    slots = slot_table(owner_map, lax.axis_index("row") * 16 + lax.axis_index("col"))
    pad = jnp.zeros((72, 14, 50), BF)
    low = jnp.concatenate([packed_store[:, 32:, :], pad], axis=1)
    packed = jnp.concatenate([packed_store[:, :32, :], low, jnp.zeros((72, 32, 28), BF)], axis=2)
    dma = pltpu.SemaphoreType.DMA
    vm = lambda *s: pltpu.VMEM(s, BF)
    return pl.pallas_call(
        kernel,
        out_shape=jax.ShapeDtypeStruct((TILE, TILE), BF),
        in_specs=[pl.BlockSpec(memory_space=pltpu.SMEM)] * 2 + [pl.BlockSpec(memory_space=pl.ANY)]
        + [pl.BlockSpec(memory_space=pltpu.VMEM)] * 2,
        out_specs=pl.BlockSpec(memory_space=pltpu.VMEM),
        scratch_shapes=[
            vm(128, 32, 128), vm(128, 32, 128),
            vm(6, KB, 384), vm(4, KB, 896), vm(6, SLOT, MAIN), vm(3, ROWS, MAIN), vm(16, ROWS, MAIN), vm(16, NROWS, NMAIN),
            vm(256, 2048), vm(2048, NPAD), vm(2048, NPAD), vm(NPAD, NPAD), vm(512, NPAD),
            pltpu.VMEM((ROWS, NPAD), F32), vm(4, 256, 256), vm(256, NPAD), pltpu.VMEM((512, 128), F32), pltpu.VMEM((512, 128), F32),
            dma((6,)), dma((4,)), dma, dma, dma,
            dma((6,)), dma((6,)), dma((3,)), dma((3,)),
            dma((6, 2, 2)), dma((6, 2, 2)), dma((6, 2)), dma((6, 2)), dma((6, 4)), dma((6, 4)), dma((1,)), dma((1,)),
            dma((19,)), dma((20,)),
        ],
        compiler_params=pltpu.CompilerParams(collective_id=1, has_side_effects=True, vmem_limit_bytes=60 * 2**20),
        cost_estimate=pl.CostEstimate(flops=2 * 800 * 800 * 6400, bytes_accessed=20_000_000, transcendentals=0),
    )(slots, owner_map, integrals.T, packed, pair_sector.reshape(50, 128))


def solution(mesh):
    in_specs = (P(None, "col"), P(("row", "col"), None, None), P(), P())
    return jax.shard_map(body, mesh=mesh, in_specs=in_specs, out_specs=P("col", "row"), check_vma=False)
```

```python
import functools

import jax
import jax.numpy as jnp
import numpy as np
from jax import lax
from jax.experimental import pallas as pl
from jax.experimental.pallas import tpu as pltpu
from jax.sharding import PartitionSpec as P

MESH = pl.DeviceIdType.MESH
BF = jnp.bfloat16
F32 = jnp.float32

TILE = 800
KB = 400
MAIN = 384
REM = 16
PIECE = 208
SLOT = PIECE + REM
ROWS = 4 * SLOT
NPAD = 896
NMAIN = 768
NROWS = KB + 32
WHOLE, LOW, HIGH = (0, NROWS), (0, 208), (208, 224)
CUTS_X = ((0, 144), (144, 144), (288, 144))
X_SEMS = ((2, 0), (17, 18), (18, 19))
SHIFTS = (1, 3, 2)
OFFS = [(dxh, dy) for dxh in range(2) for dy in SHIFTS]
LATE_XL = (4, 5)
EARLY = 2
ORDER = ('F0', 'P0', 'Y0', 'ZA0', 'P3', 'Y3', 'P1', 'S2', 'P4', 'Y1', 'ZA3', 'ZA1', 'ZA4', 'E1', 'X0', 'Y4', 'ZB0', 'E2', 'X3', 'P2', 'P5', 'X1', 'ZB3', 'ZB1', 'ZA5', 'ZA2', 'U00', 'F', 'U30', 'M00', 'X4', 'U10', 'M01', 'V40', 'U40', 'M02', 'M03', 'L', 'H', 'U01', 'U31', 'U11', 'V50', 'C', 'Y5', 'Y2', 'Q', 'U50', 'U20', 'M20', 'X5', 'X2', 'ZB2', 'M21', 'W40', 'M22', 'M23', 'M30', 'M31', 'M32', 'J', 'G', 'M33', 'U21', 'M50', 'M51', 'M52', 'M53', 'M40', 'M41', 'M42', 'W50', 'M43', 'M10', 'M11', 'M12', 'R', 'M13', 'M60', 'M61', 'M62', 'M63', 'M70', 'M71', 'M72', 'M73')


def piece_start(q):
    return 192 * q + 16 * (q // 3)


def kernel(slots, owner, integrals, packed, sector, out,
           sendbuf, fin, win, win_full, stage, stage_full, irecv, arecv,
           x_buf, e1, e2, s_buf, st_buf, acc, l_buf, arem, sec_rows, tail,
           w_sem, wf_sem, s1_send, s1_recv, own_sem, p1_send, p1_recv, full_send, full_recv,
           z_send, z_recv, z2_send, z2_recv, xl_send, xl_recv, ex_send, ex_recv, a_send, a_recv):
    r = lax.axis_index("row")
    c = lax.axis_index("col")
    z, xl = r // 2, r % 2
    xh, y, k = c // 8, (c // 2) % 4, c % 2

    def col(xh_, y_, k_):
        return xh_ * 8 + (y_ % 4) * 2 + k_

    def remote(src, dst, ssem, rsem_, row_, col_):
        return pltpu.make_async_remote_copy(src_ref=src, dst_ref=dst, send_sem=ssem, recv_sem=rsem_,
                                            device_id=(row_, col_), device_id_type=MESH)

    sends = []

    def send(cp):
        cp.start()
        sends.append(cp)

    mate = c + 1 - 2 * k
    cross_c = c + 8 - 16 * xh
    row_flip = z * 2 + 1 - xl

    me = r * 16 + c
    barrier = pltpu.get_barrier_semaphore()

    def greet(dr, carry):
        for dc in range(16):
            pl.semaphore_signal(barrier, inc=1, device_id=((r + dr) % 8, (c + dc) % 16), device_id_type=MESH)
        return carry
    for dc in range(1, 16):
        pl.semaphore_signal(barrier, inc=1, device_id=(r, (c + dc) % 16), device_id_type=MESH)
    lax.fori_loop(1, 8, greet, 0)

    dx = (k + xl) % 2
    p_xh = (xh + dx) % 2
    p_row = z * 2 + (xl + dx) % 2
    p_cols = [col(p_xh, y + dy, kk) for dy in SHIFTS for kk in range(2)]
    full_c = [mate, col(1 - xh, y, 0), col(1 - xh, y, 1), c]

    def window(start, width):
        first = jnp.minimum(start // 128, (12800 - width) // 128) * 128
        return pl.multiple_of(first, 128), start - first

    win_off, win_cp = [], []
    for n in range(6):
        w0, off = window(p_cols[n] * TILE + piece_start(z), 384)
        cp = pltpu.make_async_copy(integrals.at[:, pl.ds(w0, 384)], win.at[n], w_sem.at[n])
        cp.start()
        win_off.append(off)
        win_cp.append(cp)
    full_off, full_cp = [], []
    for f in range(4):
        w0, off = window(full_c[f] * TILE, 896)
        cp = pltpu.make_async_copy(integrals.at[:, pl.ds(w0, 896)], win_full.at[f], wf_sem.at[f])
        cp.start()
        full_off.append(off)
        full_cp.append(cp)

    def pick(n, carry):
        sendbuf[n] = packed[slots[n]]
        return carry
    lax.fori_loop(0, 128, pick, 0, unroll=8)

    def turn_piece(read, off, store):
        i = lax.broadcasted_iota(jnp.int32, (256, 384), 0)
        lane = lax.broadcasted_iota(jnp.int32, (256, 384), 1)
        pick_rows = jnp.where((i < PIECE) & (lane == i + off), 1.0, 0.0).astype(BF)
        dims = (((1,), (1,)), ((), ()))
        main = lax.dot_general(pick_rows[:PIECE], read(0, MAIN), dims, preferred_element_type=F32)
        rest = lax.dot_general(read(MAIN, REM), pick_rows, dims, preferred_element_type=F32)
        store(main.astype(BF), rest.astype(BF))

    def into(ref, row0):
        def store(main, rest):
            ref[pl.ds(row0, PIECE), :] = main
            ref[pl.ds(row0 + PIECE, REM), pl.ds(0, 256)] = rest
            ref[pl.ds(row0 + PIECE, REM), pl.ds(256, 128)] = jnp.zeros((REM, 128), BF)
        return store

    zrow = pl.multiple_of(z * SLOT, 16)

    def send_p1(i):
        for n in (2 * i, 2 * i + 1):
            send(remote(stage.at[n], irecv.at[c, pl.ds(zrow, SLOT), :], p1_send.at[n], p1_recv.at[dx * 3 + i], p_row, p_cols[n]))

    def stage_p1(n):
        win_cp[n].wait()
        turn_piece(lambda k0, kn: win[n, pl.ds(k0, kn), :], win_off[n], into(stage.at[n], 0))

    for n in range(2 * EARLY):
        stage_p1(n)
    pl.semaphore_wait(barrier, 127)
    for i in range(EARLY):
        send_p1(i)

    def give(to_r, to_c):
        to = to_r * 16 + to_c
        remote(sendbuf.at[to], fin.at[me], s1_send, s1_recv, to_r, to_c).start()

    def give_row(d, carry):
        for dc in range(16):
            give((r + d) % 8, (c + dc) % 16)
        return carry
    for dc in range(1, 16):
        give(r, (c + dc) % 16)
    lax.fori_loop(1, 8, give_row, 0)
    own1 = pltpu.make_async_copy(sendbuf.at[me], fin.at[me], own_sem)
    own1.start()
    for n in range(2 * EARLY, 6):
        stage_p1(n)

    def turn_full(f, ref):
        full_cp[f].wait()

        def one(q, carry):
            at = full_off[f] + piece_start(q)
            lane0 = jnp.minimum(at // 128, 4) * 128
            turn_piece(lambda k0, kn: win_full[f, pl.ds(k0, kn), pl.ds(pl.multiple_of(lane0, 128), 384)],
                       at - lane0, into(ref, pl.multiple_of(q * SLOT, 16)))
            return carry
        lax.fori_loop(0, 4, one, 0)

    def send_full(f):
        send(remote(stage_full.at[f], irecv.at[c], full_send.at[f],
                    full_recv.at[0] if f == 0 else full_recv.at[1 + k], r if f == 0 else row_flip, full_c[f]))

    def send_fulls():
        send_full(1)
        send_full(2)

    def prepare():
        for f in range(3):
            turn_full(f, stage_full.at[f])
        send_full(0)
        turn_full(3, irecv.at[c])
        lax.fori_loop(0, 16, table, 0)

    def table(b, carry):
        j = lax.broadcasted_iota(jnp.int32, (128, NPAD), 0)
        col_i = lax.broadcasted_iota(jnp.int32, (128, NPAD), 1) - 50 * b
        e1[pl.ds(pl.multiple_of(b * 128, 128), 128), :] = jnp.where((j < 50) & (col_i == j), 1.0, 0.0).astype(BF)
        e2[pl.ds(pl.multiple_of(b * 128, 128), 128), :] = jnp.where(
            (j >= 50) & (j < 100) & (col_i == j - 50), 1.0, 0.0).astype(BF)
        return carry
    tail[pl.ds(KB, 112), :] = jnp.zeros((112, 128), F32)
    s_buf[pl.ds(TILE, NPAD - TILE), :] = jnp.zeros((NPAD - TILE, NPAD), BF)

    def src_col(o, half):
        dxh, dy = OFFS[o]
        core = xl if half == 0 else 1 - xl
        return col(xh + dxh - 2 * xh * dxh, y + 4 - dy, core)

    up, down = ((z + 1) % 4) * 2 + xl, ((z + 3) % 4) * 2 + xl
    zrows = [pl.multiple_of(((z + d) % 4) * SLOT, 16) for d in range(4)]

    def i_slot(o, half, d):
        return irecv.at[src_col(o, half), pl.ds(zrows[d], SLOT), :]

    def i_wait(ref, sem):
        remote(ref, ref, p1_send.at[0], sem, r, c).wait_recv()

    def to_xl(o, d):
        ref = i_slot(o, 0, d)
        send(remote(ref, ref, xl_send.at[o, d], xl_recv.at[o, d], row_flip, c))

    def both_ways(o, half):
        ref = i_slot(o, half, 0)
        send(remote(ref, ref, z_send.at[o, half, 0], z_recv.at[o, half, 0], up, c))
        send(remote(ref, ref, z_send.at[o, half, 1], z_recv.at[o, half, 1], down, c))

    def shared(o):
        i_wait(i_slot(o, 0, 0), p1_recv.at[o])

    def shared_xl(o):
        i_wait(i_slot(o, 1, 0), xl_recv.at[o, 0])

    def one_end(o, half):
        d = 3 if half == 0 else 1
        ref = i_slot(o, half, d)
        i_wait(ref, z_recv.at[o, half, half])
        send(remote(ref, ref, z2_send.at[o, half], z2_recv.at[o, half], up if half == 0 else down, c))
        if o in LATE_XL:
            to_xl(o, d)

    def other_end(o, half):
        d = 1 if half == 0 else 3
        i_wait(i_slot(o, half, d), z_recv.at[o, half, 1 - half])
        if o in LATE_XL:
            to_xl(o, d)

    def far_end(o, half):
        i_wait(i_slot(o, half, 2), z2_recv.at[o, half])
        if o in LATE_XL:
            to_xl(o, 2)

    def rest_of(o):
        if o in LATE_XL:
            for d in (1, 3, 2):
                i_wait(i_slot(o, 1, d), xl_recv.at[o, d])
        else:
            other_end(o, 0)
            far_end(o, 0)
            other_end(o, 1)
            far_end(o, 1)

    def line(first, count):
        at = first // 128
        parts = [sector[pl.ds(jnp.minimum(at + i, 49), 1), :] for i in range(count)]
        flat = jnp.broadcast_to(jnp.concatenate(parts, axis=1), (8, 128 * count))
        return pltpu.roll(flat, 128 * count - (first - at * 128), axis=1)
    sec_cols = line(r * TILE, 8)[0:1, :NPAD]
    sec_rows[...] = jnp.broadcast_to(line(c * KB, 5)[0:1, :512], (128, 512)).astype(F32).T
    sec_cols = sec_cols.astype(F32)

    own_half = s_buf.at[pl.ds(pl.multiple_of(k * KB, 16), KB), :]
    mate_half = s_buf.at[pl.ds(pl.multiple_of((1 - k) * KB, 16), KB), :]

    def assemble():
        own1.wait()
        remote(sendbuf.at[pl.ds(0, 127)], fin.at[pl.ds(0, 127)], s1_send, s1_recv, r, c).wait_recv()

        def put(a, carry):
            for b in range(16):
                x_buf[pl.ds(pl.multiple_of(32 * a, 32), 32), pl.ds(128 * b, 128)] = fin[owner[16 * a + b]]
            return carry
        lax.fori_loop(0, 8, put, 0)
        m_i = lax.broadcasted_iota(jnp.int32, (KB, 256), 0)
        n_i = lax.broadcasted_iota(jnp.int32, (KB, 256), 1)
        blk = (m_i * 1311) >> 16
        inner = m_i - 50 * blk
        f1 = jnp.where((inner < 32) & (n_i == 32 * blk + inner), 1.0, 0.0).astype(BF)
        f2 = jnp.where((inner >= 32) & (n_i == 32 * blk + inner - 32), 1.0, 0.0).astype(BF)
        for n0, nw, k0, kw in ((0, 256, 0, 768), (256, 256, 640, 768), (512, 256, 1280, 768), (768, 128, 1920, 128)):
            x = x_buf[:, pl.ds(k0, kw)]
            y1 = jnp.dot(x, e1[pl.ds(k0, kw), pl.ds(n0, nw)], preferred_element_type=F32).astype(BF)
            y2 = jnp.dot(x, e2[pl.ds(k0, kw), pl.ds(n0, nw)], preferred_element_type=F32).astype(BF)
            part = jnp.dot(f1, y1, preferred_element_type=F32) + jnp.dot(f2, y2, preferred_element_type=F32)
            s_buf[pl.ds(pl.multiple_of(k * KB, 16), KB), pl.ds(n0, nw)] = part.astype(BF)
        send(remote(own_half, own_half, ex_send.at[0], ex_recv.at[0], r, mate))

    yup, ydown = col(xh, y + 1, k), col(xh, y + 3, k)

    def a_rows(cc, rows):
        return arecv.at[cc, pl.ds(rows[0], rows[1]), :]

    def a_send_to(cc, i, j, dest, rows=WHOLE):
        ref = a_rows(cc, rows)
        send(remote(ref, ref, a_send.at[i], a_recv.at[j], r, dest))

    def a_wait(cc, j, rows=WHOLE):
        ref = a_rows(cc, rows)
        remote(ref, ref, a_send.at[0], a_recv.at[j], r, c).wait_recv()

    def xy(dxh, dy, kk):
        return col(xh + dxh - 2 * xh * dxh, y + dy + 4, kk)

    def complete():
        remote(mate_half, mate_half, ex_send.at[0], ex_recv.at[0], r, c).wait_recv()

        def turn(i, carry):
            at = pl.ds(pl.multiple_of(i * 128, 128), 128)
            st_buf[:, at] = s_buf[at, pl.ds(pl.multiple_of(k * MAIN, 128), 512)].T
            return carry
        lax.fori_loop(0, 7, turn, 0)

        def choose(i, carry):
            row0 = pl.multiple_of(i * 80, 16)
            straight = s_buf[pl.ds(pl.multiple_of(k * KB + row0, 16), 80), :]
            flipped = st_buf[pl.ds(pl.multiple_of(16 * k + row0, 16), 80), :]
            g_k = lax.broadcasted_iota(jnp.int32, (80, NPAD), 0) + (c * KB + row0)
            g_n = lax.broadcasted_iota(jnp.int32, (80, NPAD), 1) + r * TILE
            tile = jnp.where(g_k <= g_n, straight.astype(F32), flipped.astype(F32))
            tile = jnp.where(sec_rows[pl.ds(row0, 80), 0:1] == sec_cols, tile, 0.0)
            arecv[c, pl.ds(row0, 80), :] = tile[:, :NMAIN].astype(BF)
            tail[pl.ds(row0, 80), :] = tile[:, NMAIN:]
            return carry
        lax.fori_loop(0, 5, choose, 0)
        arecv[c, pl.ds(KB, 32), pl.ds(0, 512)] = tail[...].T[:32].astype(BF)
        arecv[c, pl.ds(KB, 32), pl.ds(512, 256)] = jnp.zeros((32, 256), BF)
        arecv[c, pl.ds(KB, 16), pl.ds(512, 128)] = tail[pl.ds(MAIN, 16), :].astype(BF)
        for i, rows in enumerate(CUTS_X):
            a_send_to(c, X_SEMS[i][0], X_SEMS[i][1], cross_c, rows=rows)
        a_send_to(c, 0, 1, yup)
        a_send_to(c, 1, 2, ydown)
        a_send_to(c, 3, 8, mate)

    def from_x():
        for i, rows in enumerate(CUTS_X):
            a_wait(cross_c, X_SEMS[i][1], rows)
        a_send_to(cross_c, 4, 3, yup)
        a_send_to(cross_c, 5, 4, ydown)
        a_send_to(cross_c, 6, 9, mate)

    def from_y(dxh, dy, j, on, to_mate):
        cc = xy(dxh, dy, k)
        a_wait(cc, j)
        i, j2, dest, rows = on
        a_send_to(cc, i, j2, dest, rows=rows)
        a_send_to(cc, *to_mate, mate)

    def from_y2(dxh, low, high, to_mate):
        cc = xy(dxh, 2, k)
        a_wait(cc, low, LOW)
        a_wait(cc, high, HIGH)
        a_send_to(cc, *to_mate, mate)

    def product(dxh, dy, n, first):
        c0, c1 = xy(dxh, dy, 0), xy(dxh, dy, 1)

        def add(at, part):
            if first:
                acc[:, at] = part
            else:
                acc[:, at] += part

        left = jnp.concatenate([irecv[c0], irecv[c1]], axis=1)
        if n < 3:
            at = pl.ds(n * 256, 256)
            right = jnp.concatenate([arecv[c0, pl.ds(0, MAIN), at], arecv[c1, pl.ds(0, MAIN), at]], axis=0)
            add(at, jnp.dot(left, right, preferred_element_type=F32))
        else:
            side = pl.ds(KB, 32)
            right = jnp.concatenate([arecv[c0, side, pl.ds(0, MAIN)], arecv[c1, side, pl.ds(0, MAIN)]], axis=1)
            add(pl.ds(NMAIN, 32), lax.dot_general(left, right, (((1,), (1,)), ((), ())), preferred_element_type=F32))

    def whole(cc, sem):
        ref = irecv.at[cc]
        remote(ref, ref, full_send.at[0], full_recv.at[sem], r, c).wait_recv()

    def multiply(i, n, first):
        dxh, dy, j = ((0, 0, 8), (1, 0, 9), (0, -1, 10), (0, 1, 11), (1, 1, 12), (1, -1, 13), (0, 2, 14), (1, 2, 15))[i]
        if n > 0:
            product(dxh, dy, n, first)
            return
        if i == 0:
            whole(mate, 0)
        elif i == 1:
            whole(xy(1, 0, 0), 1)
            whole(xy(1, 0, 1), 2)
        else:
            rest_of(dxh * 3 + {-1: 0, 1: 1, 2: 2}[dy])
        a_wait(xy(dxh, dy, 1 - k), j)
        product(dxh, dy, n, first)

    steps = {"F": send_fulls, "F0": prepare, "E1": assemble, "E2": complete, "C": from_x}
    for i in range(3):
        steps["S%d" % i] = functools.partial(send_p1, i)
    for o in range(6):
        steps["P%d" % o] = functools.partial(shared, o)
        steps["X%d" % o] = functools.partial(shared_xl, o)
        steps["Y%d" % o] = functools.partial(to_xl, o, 0)
        steps["ZA%d" % o] = functools.partial(both_ways, o, 0)
        steps["ZB%d" % o] = functools.partial(both_ways, o, 1)
        for half in range(2):
            steps["U%d%d" % (o, half)] = functools.partial(one_end, o, half)
            steps["V%d%d" % (o, half)] = functools.partial(other_end, o, half)
            steps["W%d%d" % (o, half)] = functools.partial(far_end, o, half)
    steps["L"] = functools.partial(from_y, 0, -1, 1, (7, 5, yup, LOW), (8, 10))
    steps["H"] = functools.partial(from_y, 0, 1, 2, (15, 16, ydown, HIGH), (9, 11))
    steps["G"] = functools.partial(from_y, 1, 1, 4, (10, 6, ydown, HIGH), (11, 12))
    steps["J"] = functools.partial(from_y, 1, -1, 3, (16, 17, yup, LOW), (12, 13))
    steps["Q"] = functools.partial(from_y2, 0, 5, 16, (13, 14))
    steps["R"] = functools.partial(from_y2, 1, 17, 6, (14, 15))
    for name in ORDER:
        if name[0] == "M":
            multiply(int(name[1]), int(name[2]), name[1] == "0")
        else:
            steps[name]()

    for cc in range(16):
        arem[pl.ds(16 * cc, 16), pl.ds(0, NMAIN)] = arecv[cc, pl.ds(MAIN, REM), :]
        arem[pl.ds(16 * cc, 16), pl.ds(NMAIN, 128)] = arecv[cc, pl.ds(KB, 16), pl.ds(512, 128)]
        for q in range(4):
            l_buf[q, pl.ds(16 * cc, 16), :] = irecv[cc, pl.ds(q * SLOT + PIECE, REM), pl.ds(0, 256)]
    for q, (skip, row0) in enumerate(((0, 0), (16, 208), (16, 400), (0, 592))):
        part = lax.dot_general(l_buf[q], arem[...], (((0,), (0,)), ((), ())), preferred_element_type=F32)
        rows = PIECE - skip
        total = acc[pl.ds(q * SLOT + skip, rows), pl.ds(0, TILE)] + part[skip:PIECE, :TILE]
        out[pl.ds(row0, rows), :] = total.astype(BF)

    for cp in sends:
        cp.wait_send()
    remote(sendbuf.at[pl.ds(0, 127)], fin.at[pl.ds(0, 127)], s1_send, s1_recv, r, c).wait_send()


def slot_constants():
    table = np.zeros((128, 128), np.int32)
    for cls in range(128):
        a, b = cls // 16, cls % 16
        blocks = [(a + 8 * t, b + 16 * u) for t in range(16) for u in range(8) if a + 8 * t <= b + 16 * u]
        place = {block: i for i, block in enumerate(blocks)}
        for n in range(128):
            rr, cc = n // 16, n % 16
            lo, hi, h = min(rr, cc // 2), max(rr, cc // 2), cc % 2
            table[cls, n] = place.get((a + 8 * (2 * lo + h), b + 16 * hi), 0)
    return table


def slot_table(owner_map, me):
    return jnp.sum(jnp.where((owner_map == me)[:, None], jnp.asarray(slot_constants()), 0), axis=0)


def body(integrals, packed_store, pair_sector, owner_map):
    slots = slot_table(owner_map, lax.axis_index("row") * 16 + lax.axis_index("col"))
    pad = jnp.zeros((72, 14, 50), BF)
    low = jnp.concatenate([packed_store[:, 32:, :], pad], axis=1)
    packed = jnp.concatenate([packed_store[:, :32, :], low, jnp.zeros((72, 32, 28), BF)], axis=2)
    dma = pltpu.SemaphoreType.DMA
    vm = lambda *s: pltpu.VMEM(s, BF)
    return pl.pallas_call(
        kernel,
        out_shape=jax.ShapeDtypeStruct((TILE, TILE), BF),
        in_specs=[pl.BlockSpec(memory_space=pltpu.SMEM)] * 2 + [pl.BlockSpec(memory_space=pl.ANY)]
        + [pl.BlockSpec(memory_space=pltpu.VMEM)] * 2,
        out_specs=pl.BlockSpec(memory_space=pltpu.VMEM),
        scratch_shapes=[
            vm(128, 32, 128), vm(128, 32, 128),
            vm(6, KB, 384), vm(4, KB, 896), vm(6, SLOT, MAIN), vm(3, ROWS, MAIN), vm(16, ROWS, MAIN), vm(16, NROWS, NMAIN),
            vm(256, 2048), vm(2048, NPAD), vm(2048, NPAD), vm(NPAD, NPAD), vm(512, NPAD),
            pltpu.VMEM((ROWS, NPAD), F32), vm(4, 256, 256), vm(256, NPAD), pltpu.VMEM((512, 128), F32), pltpu.VMEM((512, 128), F32),
            dma((6,)), dma((4,)), dma, dma, dma,
            dma((6,)), dma((6,)), dma((3,)), dma((3,)),
            dma((6, 2, 2)), dma((6, 2, 2)), dma((6, 2)), dma((6, 2)), dma((6, 4)), dma((6, 4)), dma((1,)), dma((1,)),
            dma((19,)), dma((20,)),
        ],
        compiler_params=pltpu.CompilerParams(collective_id=1, has_side_effects=True, vmem_limit_bytes=60 * 2**20),
        cost_estimate=pl.CostEstimate(flops=2 * 800 * 800 * 6400, bytes_accessed=20_000_000, transcendentals=0),
    )(slots, owner_map, integrals.T, packed, pair_sector.reshape(50, 128))


def solution(mesh):
    in_specs = (P(None, "col"), P(("row", "col"), None, None), P(), P())
    return jax.shard_map(body, mesh=mesh, in_specs=in_specs, out_specs=P("col", "row"), check_vma=False)
```

```python
import functools

import jax
import jax.numpy as jnp
import numpy as np
from jax import lax
from jax.experimental import pallas as pl
from jax.experimental.pallas import tpu as pltpu
from jax.sharding import PartitionSpec as P

MESH = pl.DeviceIdType.MESH
BF = jnp.bfloat16
F32 = jnp.float32

TILE = 800
KB = 400
MAIN = 384
REM = 16
PIECE = 208
SLOT = PIECE + REM
ROWS = 4 * SLOT
NPAD = 896
NMAIN = 768
NROWS = KB + 32
WHOLE, LOW, HIGH = (0, NROWS), (0, 208), (208, 224)
CUTS_X = ((0, 144), (144, 144), (288, 144))
X_SEMS = ((2, 0), (17, 18), (18, 19))
SHIFTS = (1, 3, 2)
OFFS = [(dxh, dy) for dxh in range(2) for dy in SHIFTS]
LATE_XL = (4, 5)
EARLY = 2
ORDER = ('F0', 'P0', 'Y0', 'ZA0', 'P3', 'Y3', 'P1', 'S2', 'P4', 'Y1', 'ZA3', 'ZA1', 'ZA4', 'E1', 'X0', 'Y4', 'ZB0', 'E2', 'X3', 'P2', 'P5', 'X1', 'ZB3', 'ZB1', 'ZA5', 'ZA2', 'U00', 'F', 'U30', 'M00', 'X4', 'U10', 'M01', 'V40', 'U40', 'M02', 'M03', 'L', 'H', 'U01', 'U31', 'U11', 'V50', 'C', 'Y5', 'Y2', 'Q', 'U50', 'U20', 'M20', 'X5', 'X2', 'ZB2', 'M21', 'W40', 'M22', 'M23', 'M30', 'M31', 'M32', 'J', 'G', 'M33', 'U21', 'M50', 'M51', 'M52', 'M53', 'M40', 'M41', 'M42', 'W50', 'M43', 'M10', 'M11', 'M12', 'R', 'M13', 'M60', 'M61', 'M62', 'M63', 'M70', 'M71', 'M72', 'M73')


def piece_start(q):
    return 192 * q + 16 * (q // 3)


def kernel(slots, owner, integrals, packed, sector, out,
           sendbuf, fin, win, win_full, stage, stage_full, irecv, arecv,
           x_buf, e1, e2, s_buf, st_buf, acc, l_buf, arem, sec_rows, tail,
           w_sem, wf_sem, s1_send, s1_recv, own_sem, p1_send, p1_recv, full_send, full_recv,
           z_send, z_recv, z2_send, z2_recv, xl_send, xl_recv, ex_send, ex_recv, a_send, a_recv):
    r = lax.axis_index("row")
    c = lax.axis_index("col")
    z, xl = r // 2, r % 2
    xh, y, k = c // 8, (c // 2) % 4, c % 2

    def col(xh_, y_, k_):
        return xh_ * 8 + (y_ % 4) * 2 + k_

    def remote(src, dst, ssem, rsem_, row_, col_):
        return pltpu.make_async_remote_copy(src_ref=src, dst_ref=dst, send_sem=ssem, recv_sem=rsem_,
                                            device_id=(row_, col_), device_id_type=MESH)

    sends = []

    def send(cp):
        cp.start()
        sends.append(cp)

    mate = c + 1 - 2 * k
    cross_c = c + 8 - 16 * xh
    row_flip = z * 2 + 1 - xl

    me = r * 16 + c
    barrier = pltpu.get_barrier_semaphore()

    def greet(dr, carry):
        for dc in range(16):
            pl.semaphore_signal(barrier, inc=1, device_id=((r + dr) % 8, (c + dc) % 16), device_id_type=MESH)
        return carry
    for dc in range(1, 16):
        pl.semaphore_signal(barrier, inc=1, device_id=(r, (c + dc) % 16), device_id_type=MESH)
    lax.fori_loop(1, 8, greet, 0)

    dx = (k + xl) % 2
    p_xh = (xh + dx) % 2
    p_row = z * 2 + (xl + dx) % 2
    p_cols = [col(p_xh, y + dy, kk) for dy in SHIFTS for kk in range(2)]
    full_c = [mate, col(1 - xh, y, 0), col(1 - xh, y, 1), c]

    def window(start, width):
        first = jnp.minimum(start // 128, (12800 - width) // 128) * 128
        return pl.multiple_of(first, 128), start - first

    win_off, win_cp = [], []
    for n in range(6):
        w0, off = window(p_cols[n] * TILE + piece_start(z), 384)
        cp = pltpu.make_async_copy(integrals.at[:, pl.ds(w0, 384)], win.at[n], w_sem.at[n])
        cp.start()
        win_off.append(off)
        win_cp.append(cp)
    full_off, full_cp = [], []
    for f in range(4):
        w0, off = window(full_c[f] * TILE, 896)
        cp = pltpu.make_async_copy(integrals.at[:, pl.ds(w0, 896)], win_full.at[f], wf_sem.at[f])
        cp.start()
        full_off.append(off)
        full_cp.append(cp)

    def pick(n, carry):
        sendbuf[n] = packed[slots[n]]
        return carry
    lax.fori_loop(0, 128, pick, 0, unroll=8)

    def turn_piece(read, off, store):
        i = lax.broadcasted_iota(jnp.int32, (256, 384), 0)
        lane = lax.broadcasted_iota(jnp.int32, (256, 384), 1)
        pick_rows = jnp.where((i < PIECE) & (lane == i + off), 1.0, 0.0).astype(BF)
        dims = (((1,), (1,)), ((), ()))
        main = lax.dot_general(pick_rows[:PIECE], read(0, MAIN), dims, preferred_element_type=F32)
        rest = lax.dot_general(read(MAIN, REM), pick_rows, dims, preferred_element_type=F32)
        store(main.astype(BF), rest.astype(BF))

    def into(ref, row0):
        def store(main, rest):
            ref[pl.ds(row0, PIECE), :] = main
            ref[pl.ds(row0 + PIECE, REM), pl.ds(0, 256)] = rest
            ref[pl.ds(row0 + PIECE, REM), pl.ds(256, 128)] = jnp.zeros((REM, 128), BF)
        return store

    zrow = pl.multiple_of(z * SLOT, 16)

    def send_p1(i):
        for n in (2 * i, 2 * i + 1):
            send(remote(stage.at[n], irecv.at[c, pl.ds(zrow, SLOT), :], p1_send.at[n], p1_recv.at[dx * 3 + i], p_row, p_cols[n]))

    def stage_p1(n):
        win_cp[n].wait()
        turn_piece(lambda k0, kn: win[n, pl.ds(k0, kn), :], win_off[n], into(stage.at[n], 0))

    for n in range(2 * EARLY):
        stage_p1(n)
    pl.semaphore_wait(barrier, 127)
    for i in range(EARLY):
        send_p1(i)

    def give(to_r, to_c):
        to = to_r * 16 + to_c
        remote(sendbuf.at[to], fin.at[me], s1_send, s1_recv, to_r, to_c).start()

    def give_row(d, carry):
        for dc in range(16):
            give((r + d) % 8, (c + dc) % 16)
        return carry
    for dc in range(1, 16):
        give(r, (c + dc) % 16)
    lax.fori_loop(1, 8, give_row, 0)
    own1 = pltpu.make_async_copy(sendbuf.at[me], fin.at[me], own_sem)
    own1.start()
    for n in range(2 * EARLY, 6):
        stage_p1(n)

    def turn_full(f, ref):
        full_cp[f].wait()

        def one(q, carry):
            at = full_off[f] + piece_start(q)
            lane0 = jnp.minimum(at // 128, 4) * 128
            turn_piece(lambda k0, kn: win_full[f, pl.ds(k0, kn), pl.ds(pl.multiple_of(lane0, 128), 384)],
                       at - lane0, into(ref, pl.multiple_of(q * SLOT, 16)))
            return carry
        lax.fori_loop(0, 4, one, 0)

    def send_full(f):
        send(remote(stage_full.at[f], irecv.at[c], full_send.at[f],
                    full_recv.at[0] if f == 0 else full_recv.at[1 + k], r if f == 0 else row_flip, full_c[f]))

    def send_fulls():
        send_full(1)
        send_full(2)

    def prepare():
        for f in range(3):
            turn_full(f, stage_full.at[f])
        send_full(0)
        turn_full(3, irecv.at[c])
        lax.fori_loop(0, 16, table, 0)

    def table(b, carry):
        j = lax.broadcasted_iota(jnp.int32, (128, NPAD), 0)
        col_i = lax.broadcasted_iota(jnp.int32, (128, NPAD), 1) - 50 * b
        e1[pl.ds(pl.multiple_of(b * 128, 128), 128), :] = jnp.where((j < 50) & (col_i == j), 1.0, 0.0).astype(BF)
        e2[pl.ds(pl.multiple_of(b * 128, 128), 128), :] = jnp.where(
            (j >= 50) & (j < 100) & (col_i == j - 50), 1.0, 0.0).astype(BF)
        return carry
    tail[pl.ds(KB, 112), :] = jnp.zeros((112, 128), F32)
    s_buf[pl.ds(TILE, NPAD - TILE), :] = jnp.zeros((NPAD - TILE, NPAD), BF)

    def src_col(o, half):
        dxh, dy = OFFS[o]
        core = xl if half == 0 else 1 - xl
        return col(xh + dxh - 2 * xh * dxh, y + 4 - dy, core)

    up, down = ((z + 1) % 4) * 2 + xl, ((z + 3) % 4) * 2 + xl
    zrows = [pl.multiple_of(((z + d) % 4) * SLOT, 16) for d in range(4)]

    def i_slot(o, half, d):
        return irecv.at[src_col(o, half), pl.ds(zrows[d], SLOT), :]

    def i_wait(ref, sem):
        remote(ref, ref, p1_send.at[0], sem, r, c).wait_recv()

    def to_xl(o, d):
        ref = i_slot(o, 0, d)
        send(remote(ref, ref, xl_send.at[o, d], xl_recv.at[o, d], row_flip, c))

    def both_ways(o, half):
        ref = i_slot(o, half, 0)
        send(remote(ref, ref, z_send.at[o, half, 0], z_recv.at[o, half, 0], up, c))
        send(remote(ref, ref, z_send.at[o, half, 1], z_recv.at[o, half, 1], down, c))

    def shared(o):
        i_wait(i_slot(o, 0, 0), p1_recv.at[o])

    def shared_xl(o):
        i_wait(i_slot(o, 1, 0), xl_recv.at[o, 0])

    def one_end(o, half):
        d = 3 if half == 0 else 1
        ref = i_slot(o, half, d)
        i_wait(ref, z_recv.at[o, half, half])
        send(remote(ref, ref, z2_send.at[o, half], z2_recv.at[o, half], up if half == 0 else down, c))
        if o in LATE_XL:
            to_xl(o, d)

    def other_end(o, half):
        d = 1 if half == 0 else 3
        i_wait(i_slot(o, half, d), z_recv.at[o, half, 1 - half])
        if o in LATE_XL:
            to_xl(o, d)

    def far_end(o, half):
        i_wait(i_slot(o, half, 2), z2_recv.at[o, half])
        if o in LATE_XL:
            to_xl(o, 2)

    def rest_of(o):
        if o in LATE_XL:
            for d in (1, 3, 2):
                i_wait(i_slot(o, 1, d), xl_recv.at[o, d])
        else:
            other_end(o, 0)
            far_end(o, 0)
            other_end(o, 1)
            far_end(o, 1)

    def line(first, count):
        at = first // 128
        parts = [sector[pl.ds(jnp.minimum(at + i, 49), 1), :] for i in range(count)]
        flat = jnp.broadcast_to(jnp.concatenate(parts, axis=1), (8, 128 * count))
        return pltpu.roll(flat, 128 * count - (first - at * 128), axis=1)
    sec_cols = line(r * TILE, 8)[0:1, :NPAD]
    sec_rows[...] = jnp.broadcast_to(line(c * KB, 5)[0:1, :512], (128, 512)).astype(F32).T
    sec_cols = sec_cols.astype(F32)

    own_half = s_buf.at[pl.ds(pl.multiple_of(k * KB, 16), KB), :]
    mate_half = s_buf.at[pl.ds(pl.multiple_of((1 - k) * KB, 16), KB), :]

    def assemble():
        own1.wait()
        remote(sendbuf.at[pl.ds(0, 127)], fin.at[pl.ds(0, 127)], s1_send, s1_recv, r, c).wait_recv()

        def put(a, carry):
            for b in range(16):
                x_buf[pl.ds(pl.multiple_of(32 * a, 32), 32), pl.ds(128 * b, 128)] = fin[owner[16 * a + b]]
            return carry
        lax.fori_loop(0, 8, put, 0)
        m_i = lax.broadcasted_iota(jnp.int32, (KB, 256), 0)
        n_i = lax.broadcasted_iota(jnp.int32, (KB, 256), 1)
        blk = (m_i * 1311) >> 16
        inner = m_i - 50 * blk
        f1 = jnp.where((inner < 32) & (n_i == 32 * blk + inner), 1.0, 0.0).astype(BF)
        f2 = jnp.where((inner >= 32) & (n_i == 32 * blk + inner - 32), 1.0, 0.0).astype(BF)
        for n0, nw, k0, kw in ((0, 256, 0, 768), (256, 256, 640, 768), (512, 256, 1280, 768), (768, 128, 1920, 128)):
            x = x_buf[:, pl.ds(k0, kw)]
            y1 = jnp.dot(x, e1[pl.ds(k0, kw), pl.ds(n0, nw)], preferred_element_type=F32).astype(BF)
            y2 = jnp.dot(x, e2[pl.ds(k0, kw), pl.ds(n0, nw)], preferred_element_type=F32).astype(BF)
            part = jnp.dot(f1, y1, preferred_element_type=F32) + jnp.dot(f2, y2, preferred_element_type=F32)
            s_buf[pl.ds(pl.multiple_of(k * KB, 16), KB), pl.ds(n0, nw)] = part.astype(BF)
        send(remote(own_half, own_half, ex_send.at[0], ex_recv.at[0], r, mate))

    yup, ydown = col(xh, y + 1, k), col(xh, y + 3, k)

    def a_rows(cc, rows):
        return arecv.at[cc, pl.ds(rows[0], rows[1]), :]

    def a_send_to(cc, i, j, dest, rows=WHOLE):
        ref = a_rows(cc, rows)
        send(remote(ref, ref, a_send.at[i], a_recv.at[j], r, dest))

    def a_wait(cc, j, rows=WHOLE):
        ref = a_rows(cc, rows)
        remote(ref, ref, a_send.at[0], a_recv.at[j], r, c).wait_recv()

    def xy(dxh, dy, kk):
        return col(xh + dxh - 2 * xh * dxh, y + dy + 4, kk)

    def complete():
        remote(mate_half, mate_half, ex_send.at[0], ex_recv.at[0], r, c).wait_recv()

        def turn(i, carry):
            at = pl.ds(pl.multiple_of(i * 128, 128), 128)
            st_buf[:, at] = s_buf[at, pl.ds(pl.multiple_of(k * MAIN, 128), 512)].T
            return carry
        lax.fori_loop(0, 7, turn, 0)

        def choose(i, carry):
            row0 = pl.multiple_of(i * 80, 16)
            straight = s_buf[pl.ds(pl.multiple_of(k * KB + row0, 16), 80), :]
            flipped = st_buf[pl.ds(pl.multiple_of(16 * k + row0, 16), 80), :]
            g_k = lax.broadcasted_iota(jnp.int32, (80, NPAD), 0) + (c * KB + row0)
            g_n = lax.broadcasted_iota(jnp.int32, (80, NPAD), 1) + r * TILE
            tile = jnp.where(g_k <= g_n, straight.astype(F32), flipped.astype(F32))
            tile = jnp.where(sec_rows[pl.ds(row0, 80), 0:1] == sec_cols, tile, 0.0)
            arecv[c, pl.ds(row0, 80), :] = tile[:, :NMAIN].astype(BF)
            tail[pl.ds(row0, 80), :] = tile[:, NMAIN:]
            return carry
        lax.fori_loop(0, 5, choose, 0)
        arecv[c, pl.ds(KB, 32), pl.ds(0, 512)] = tail[...].T[:32].astype(BF)
        arecv[c, pl.ds(KB, 32), pl.ds(512, 256)] = jnp.zeros((32, 256), BF)
        arecv[c, pl.ds(KB, 16), pl.ds(512, 128)] = tail[pl.ds(MAIN, 16), :].astype(BF)
        for i, rows in enumerate(CUTS_X):
            a_send_to(c, X_SEMS[i][0], X_SEMS[i][1], cross_c, rows=rows)
        a_send_to(c, 0, 1, yup)
        a_send_to(c, 1, 2, ydown)
        a_send_to(c, 3, 8, mate)

    def from_x():
        for i, rows in enumerate(CUTS_X):
            a_wait(cross_c, X_SEMS[i][1], rows)
        a_send_to(cross_c, 4, 3, yup)
        a_send_to(cross_c, 5, 4, ydown)
        a_send_to(cross_c, 6, 9, mate)

    def from_y(dxh, dy, j, on, to_mate):
        cc = xy(dxh, dy, k)
        a_wait(cc, j)
        i, j2, dest, rows = on
        a_send_to(cc, i, j2, dest, rows=rows)
        a_send_to(cc, *to_mate, mate)

    def from_y2(dxh, low, high, to_mate):
        cc = xy(dxh, 2, k)
        a_wait(cc, low, LOW)
        a_wait(cc, high, HIGH)
        a_send_to(cc, *to_mate, mate)

    def product(dxh, dy, n, first):
        c0, c1 = xy(dxh, dy, 0), xy(dxh, dy, 1)

        def add(at, part):
            if first:
                acc[:, at] = part
            else:
                acc[:, at] += part

        left = jnp.concatenate([irecv[c0], irecv[c1]], axis=1)
        if n < 3:
            at = pl.ds(n * 256, 256)
            right = jnp.concatenate([arecv[c0, pl.ds(0, MAIN), at], arecv[c1, pl.ds(0, MAIN), at]], axis=0)
            add(at, jnp.dot(left, right, preferred_element_type=F32))
        else:
            side = pl.ds(KB, 32)
            right = jnp.concatenate([arecv[c0, side, pl.ds(0, MAIN)], arecv[c1, side, pl.ds(0, MAIN)]], axis=1)
            add(pl.ds(NMAIN, 32), lax.dot_general(left, right, (((1,), (1,)), ((), ())), preferred_element_type=F32))

    def whole(cc, sem):
        ref = irecv.at[cc]
        remote(ref, ref, full_send.at[0], full_recv.at[sem], r, c).wait_recv()

    def multiply(i, n, first):
        dxh, dy, j = ((0, 0, 8), (1, 0, 9), (0, -1, 10), (0, 1, 11), (1, 1, 12), (1, -1, 13), (0, 2, 14), (1, 2, 15))[i]
        if n > 0:
            product(dxh, dy, n, first)
            return
        if i == 0:
            whole(mate, 0)
        elif i == 1:
            whole(xy(1, 0, 0), 1)
            whole(xy(1, 0, 1), 2)
        else:
            rest_of(dxh * 3 + {-1: 0, 1: 1, 2: 2}[dy])
        a_wait(xy(dxh, dy, 1 - k), j)
        product(dxh, dy, n, first)

    steps = {"F": send_fulls, "F0": prepare, "E1": assemble, "E2": complete, "C": from_x}
    for i in range(3):
        steps["S%d" % i] = functools.partial(send_p1, i)
    for o in range(6):
        steps["P%d" % o] = functools.partial(shared, o)
        steps["X%d" % o] = functools.partial(shared_xl, o)
        steps["Y%d" % o] = functools.partial(to_xl, o, 0)
        steps["ZA%d" % o] = functools.partial(both_ways, o, 0)
        steps["ZB%d" % o] = functools.partial(both_ways, o, 1)
        for half in range(2):
            steps["U%d%d" % (o, half)] = functools.partial(one_end, o, half)
            steps["V%d%d" % (o, half)] = functools.partial(other_end, o, half)
            steps["W%d%d" % (o, half)] = functools.partial(far_end, o, half)
    steps["L"] = functools.partial(from_y, 0, -1, 1, (7, 5, yup, LOW), (8, 10))
    steps["H"] = functools.partial(from_y, 0, 1, 2, (15, 16, ydown, HIGH), (9, 11))
    steps["G"] = functools.partial(from_y, 1, 1, 4, (10, 6, ydown, HIGH), (11, 12))
    steps["J"] = functools.partial(from_y, 1, -1, 3, (16, 17, yup, LOW), (12, 13))
    steps["Q"] = functools.partial(from_y2, 0, 5, 16, (13, 14))
    steps["R"] = functools.partial(from_y2, 1, 17, 6, (14, 15))
    for name in ORDER:
        if name[0] == "M":
            multiply(int(name[1]), int(name[2]), name[1] == "0")
        else:
            steps[name]()

    for cc in range(16):
        arem[pl.ds(16 * cc, 16), pl.ds(0, NMAIN)] = arecv[cc, pl.ds(MAIN, REM), :]
        arem[pl.ds(16 * cc, 16), pl.ds(NMAIN, 128)] = arecv[cc, pl.ds(KB, 16), pl.ds(512, 128)]
        for q in range(4):
            l_buf[q, pl.ds(16 * cc, 16), :] = irecv[cc, pl.ds(q * SLOT + PIECE, REM), pl.ds(0, 256)]
    for q, (skip, row0) in enumerate(((0, 0), (16, 208), (16, 400), (0, 592))):
        part = lax.dot_general(l_buf[q], arem[...], (((0,), (0,)), ((), ())), preferred_element_type=F32)
        rows = PIECE - skip
        total = acc[pl.ds(q * SLOT + skip, rows), pl.ds(0, TILE)] + part[skip:PIECE, :TILE]
        out[pl.ds(row0, rows), :] = total.astype(BF)

    for cp in sends:
        cp.wait_send()
    remote(sendbuf.at[pl.ds(0, 127)], fin.at[pl.ds(0, 127)], s1_send, s1_recv, r, c).wait_send()


def slot_constants():
    table = np.zeros((128, 128), np.int32)
    for cls in range(128):
        a, b = cls // 16, cls % 16
        blocks = [(a + 8 * t, b + 16 * u) for t in range(16) for u in range(8) if a + 8 * t <= b + 16 * u]
        place = {block: i for i, block in enumerate(blocks)}
        for n in range(128):
            rr, cc = n // 16, n % 16
            lo, hi, h = min(rr, cc // 2), max(rr, cc // 2), cc % 2
            table[cls, n] = place.get((a + 8 * (2 * lo + h), b + 16 * hi), 0)
    return table


def slot_table(owner_map, me):
    return jnp.sum(jnp.where((owner_map == me)[:, None], jnp.asarray(slot_constants()), 0), axis=0)


def body(integrals, packed_store, pair_sector, owner_map):
    slots = slot_table(owner_map, lax.axis_index("row") * 16 + lax.axis_index("col"))
    packed = (jnp.pad(packed_store[:, :32], ((0, 0), (0, 0), (0, 78)))
              + jnp.pad(packed_store[:, 32:], ((0, 0), (0, 14), (50, 28))))
    dma = pltpu.SemaphoreType.DMA
    vm = lambda *s: pltpu.VMEM(s, BF)
    return pl.pallas_call(
        kernel,
        out_shape=jax.ShapeDtypeStruct((TILE, TILE), BF),
        in_specs=[pl.BlockSpec(memory_space=pltpu.SMEM)] * 2 + [pl.BlockSpec(memory_space=pl.ANY)]
        + [pl.BlockSpec(memory_space=pltpu.VMEM)] * 2,
        out_specs=pl.BlockSpec(memory_space=pltpu.VMEM),
        scratch_shapes=[
            vm(128, 32, 128), vm(128, 32, 128),
            vm(6, KB, 384), vm(4, KB, 896), vm(6, SLOT, MAIN), vm(3, ROWS, MAIN), vm(16, ROWS, MAIN), vm(16, NROWS, NMAIN),
            vm(256, 2048), vm(2048, NPAD), vm(2048, NPAD), vm(NPAD, NPAD), vm(512, NPAD),
            pltpu.VMEM((ROWS, NPAD), F32), vm(4, 256, 256), vm(256, NPAD), pltpu.VMEM((512, 128), F32), pltpu.VMEM((512, 128), F32),
            dma((6,)), dma((4,)), dma, dma, dma,
            dma((6,)), dma((6,)), dma((3,)), dma((3,)),
            dma((6, 2, 2)), dma((6, 2, 2)), dma((6, 2)), dma((6, 2)), dma((6, 4)), dma((6, 4)), dma((1,)), dma((1,)),
            dma((19,)), dma((20,)),
        ],
        compiler_params=pltpu.CompilerParams(collective_id=1, has_side_effects=True, vmem_limit_bytes=60 * 2**20),
        cost_estimate=pl.CostEstimate(flops=2 * 800 * 800 * 6400, bytes_accessed=20_000_000, transcendentals=0),
    )(slots, owner_map, integrals.T, packed, pair_sector.reshape(50, 128))


def solution(mesh):
    in_specs = (P(None, "col"), P(("row", "col"), None, None), P(), P())
    return jax.shard_map(body, mesh=mesh, in_specs=in_specs, out_specs=P("col", "row"), check_vma=False)
```

```python
import functools

import jax
import jax.numpy as jnp
import numpy as np
from jax import lax
from jax.experimental import pallas as pl
from jax.experimental.pallas import tpu as pltpu
from jax.sharding import PartitionSpec as P

MESH = pl.DeviceIdType.MESH
BF = jnp.bfloat16
F32 = jnp.float32

TILE = 800
KB = 400
MAIN = 384
REM = 16
PIECE = 208
SLOT = PIECE + REM
ROWS = 4 * SLOT
NPAD = 896
NMAIN = 768
NROWS = KB + 32
WHOLE, LOW, HIGH = (0, NROWS), (0, 208), (208, 224)
CUTS_X = ((0, 144), (144, 144), (288, 144))
X_SEMS = ((2, 0), (17, 18), (18, 19))
SHIFTS = (1, 3, 2)
OFFS = [(dxh, dy) for dxh in range(2) for dy in SHIFTS]
LATE_XL = (4,)
EARLY = 2
ORDER = ('F0', 'P0', 'Y0', 'ZA0', 'P3', 'ZA3', 'P1', 'ZA1', 'P4', 'ZA4', 'X0', 'Y3', 'ZB0', 'E1', 'S2', 'X3', 'Y1', 'E2', 'F', 'M00', 'M01', 'M02', 'U00', 'ZB3', 'U30', 'P2', 'ZA2', 'P5', 'U10', 'ZA5', 'X1', 'Y2', 'V40', 'U40', 'ZB1', 'U01', 'M03', 'L', 'H', 'U31', 'C', 'U11', 'X2', 'Y5', 'ZB2', 'Q', 'X5', 'Y4', 'ZB5', 'M20', 'M21', 'M22', 'M23', 'U20', 'U50', 'W40', 'U21', 'X4', 'M30', 'M31', 'M32', 'M33', 'U51', 'J', 'G', 'M50', 'M51', 'M52', 'M53', 'M40', 'M41', 'M42', 'M43', 'M10', 'M11', 'M12', 'M13', 'R', 'M60', 'M61', 'M62', 'M63', 'M70', 'M71', 'M72', 'M73')


def piece_start(q):
    return 192 * q + 16 * (q // 3)


def kernel(slots, owner, integrals, packed, sector, out,
           sendbuf, fin, win, win_full, stage, stage_full, irecv, arecv,
           x_buf, e1, e2, s_buf, st_buf, acc, l_buf, arem, sec_rows, tail,
           all_sem, w_sem, wf_sem, s1_send, s1_recv, own_sem, p1_send, p1_recv, full_send, full_recv,
           z_send, z_recv, z2_send, z2_recv, xl_send, xl_recv, ex_send, ex_recv, a_send, a_recv):
    r = lax.axis_index("row")
    c = lax.axis_index("col")
    z, xl = r // 2, r % 2
    xh, y, k = c // 8, (c // 2) % 4, c % 2

    def col(xh_, y_, k_):
        return xh_ * 8 + (y_ % 4) * 2 + k_

    def remote(src, dst, ssem, rsem_, row_, col_):
        return pltpu.make_async_remote_copy(src_ref=src, dst_ref=dst, send_sem=ssem, recv_sem=rsem_,
                                            device_id=(row_, col_), device_id_type=MESH)

    sends = []

    def send(cp):
        cp.start()
        sends.append(cp)

    mate = c + 1 - 2 * k
    cross_c = c + 8 - 16 * xh
    row_flip = z * 2 + 1 - xl

    me = r * 16 + c
    barrier = pltpu.get_barrier_semaphore()

    def greet(row_, col_):
        pl.semaphore_signal(barrier, inc=1, device_id=(row_, col_), device_id_type=MESH)

    for d in range(1, 16):
        greet(r, (c + d) % 16)
    for d in range(1, 8):
        greet((r + d) % 8, c)
    for d in range(8):
        greet(z * 2 + 1 - xl, (1 - xh) * 8 + d)

    dx = (k + xl) % 2
    p_xh = (xh + dx) % 2
    p_row = z * 2 + (xl + dx) % 2
    p_cols = [col(p_xh, y + dy, kk) for dy in SHIFTS for kk in range(2)]
    full_c = [mate, col(1 - xh, y, 0), col(1 - xh, y, 1), c]

    def window(start, width):
        first = jnp.minimum(start // 128, (12800 - width) // 128) * 128
        return pl.multiple_of(first, 128), start - first

    win_off, win_cp = [], []
    for n in range(6):
        w0, off = window(p_cols[n] * TILE + piece_start(z), 384)
        cp = pltpu.make_async_copy(integrals.at[:, pl.ds(w0, 384)], win.at[n], w_sem.at[n])
        cp.start()
        win_off.append(off)
        win_cp.append(cp)
    full_off, full_cp = [], []
    for f in range(4):
        w0, off = window(full_c[f] * TILE, 896)
        cp = pltpu.make_async_copy(integrals.at[:, pl.ds(w0, 896)], win_full.at[f], wf_sem.at[f])
        cp.start()
        full_off.append(off)
        full_cp.append(cp)

    def turn_piece(read, off, store):
        i = lax.broadcasted_iota(jnp.int32, (256, 384), 0)
        lane = lax.broadcasted_iota(jnp.int32, (256, 384), 1)
        pick_rows = jnp.where((i < PIECE) & (lane == i + off), 1.0, 0.0).astype(BF)
        dims = (((1,), (1,)), ((), ()))
        main = lax.dot_general(pick_rows[:PIECE], read(0, MAIN), dims, preferred_element_type=F32)
        rest = lax.dot_general(read(MAIN, REM), pick_rows, dims, preferred_element_type=F32)
        store(main.astype(BF), rest.astype(BF))

    def into(ref, row0):
        def store(main, rest):
            ref[pl.ds(row0, PIECE), :] = main
            ref[pl.ds(row0 + PIECE, REM), pl.ds(0, 256)] = rest
            ref[pl.ds(row0 + PIECE, REM), pl.ds(256, 128)] = jnp.zeros((REM, 128), BF)
        return store

    zrow = pl.multiple_of(z * SLOT, 16)

    def send_p1(i):
        for n in (2 * i, 2 * i + 1):
            send(remote(stage.at[n], irecv.at[c, pl.ds(zrow, SLOT), :], p1_send.at[n], p1_recv.at[dx * 3 + i], p_row, p_cols[n]))

    def stage_p1(n):
        win_cp[n].wait()
        turn_piece(lambda k0, kn: win[n, pl.ds(k0, kn), :], win_off[n], into(stage.at[n], 0))

    for n in range(2 * EARLY):
        stage_p1(n)
    pl.semaphore_wait(barrier, 30)
    for d in range(1, 8):
        pl.semaphore_signal(all_sem, inc=1, device_id=((r + d) % 8, c), device_id_type=MESH)
    for i in range(EARLY):
        send_p1(i)

    def pick(n, carry):
        sendbuf[n] = packed[slots[n]]
        return carry
    lax.fori_loop(0, 128, pick, 0, unroll=8)

    pl.semaphore_wait(all_sem, 7)

    def give(to_r, to_c):
        to = to_r * 16 + to_c
        remote(sendbuf.at[to], fin.at[me], s1_send, s1_recv, to_r, to_c).start()

    def give_row(d, carry):
        for dc in range(16):
            give((r + d) % 8, (c + dc) % 16)
        return carry
    for dc in range(1, 16):
        give(r, (c + dc) % 16)
    lax.fori_loop(1, 8, give_row, 0)
    own1 = pltpu.make_async_copy(sendbuf.at[me], fin.at[me], own_sem)
    own1.start()
    for n in range(2 * EARLY, 6):
        stage_p1(n)

    def turn_full(f, ref):
        full_cp[f].wait()

        def one(q, carry):
            at = full_off[f] + piece_start(q)
            lane0 = jnp.minimum(at // 128, 4) * 128
            turn_piece(lambda k0, kn: win_full[f, pl.ds(k0, kn), pl.ds(pl.multiple_of(lane0, 128), 384)],
                       at - lane0, into(ref, pl.multiple_of(q * SLOT, 16)))
            return carry
        lax.fori_loop(0, 4, one, 0)

    def send_full(f):
        send(remote(stage_full.at[f], irecv.at[c], full_send.at[f],
                    full_recv.at[0] if f == 0 else full_recv.at[1 + k], r if f == 0 else row_flip, full_c[f]))

    def send_fulls():
        send_full(1)
        send_full(2)

    def prepare():
        for f in range(3):
            turn_full(f, stage_full.at[f])
        send_full(0)
        turn_full(3, irecv.at[c])
        lax.fori_loop(0, 16, table, 0)

    def table(b, carry):
        j = lax.broadcasted_iota(jnp.int32, (128, NPAD), 0)
        col_i = lax.broadcasted_iota(jnp.int32, (128, NPAD), 1) - 50 * b
        e1[pl.ds(pl.multiple_of(b * 128, 128), 128), :] = jnp.where((j < 50) & (col_i == j), 1.0, 0.0).astype(BF)
        e2[pl.ds(pl.multiple_of(b * 128, 128), 128), :] = jnp.where(
            (j >= 50) & (j < 100) & (col_i == j - 50), 1.0, 0.0).astype(BF)
        return carry
    tail[pl.ds(KB, 112), :] = jnp.zeros((112, 128), F32)
    s_buf[pl.ds(TILE, NPAD - TILE), :] = jnp.zeros((NPAD - TILE, NPAD), BF)

    def src_col(o, half):
        dxh, dy = OFFS[o]
        core = xl if half == 0 else 1 - xl
        return col(xh + dxh - 2 * xh * dxh, y + 4 - dy, core)

    up, down = ((z + 1) % 4) * 2 + xl, ((z + 3) % 4) * 2 + xl
    zrows = [pl.multiple_of(((z + d) % 4) * SLOT, 16) for d in range(4)]

    def i_slot(o, half, d):
        return irecv.at[src_col(o, half), pl.ds(zrows[d], SLOT), :]

    def i_wait(ref, sem):
        remote(ref, ref, p1_send.at[0], sem, r, c).wait_recv()

    def to_xl(o, d):
        ref = i_slot(o, 0, d)
        send(remote(ref, ref, xl_send.at[o, d], xl_recv.at[o, d], row_flip, c))

    def both_ways(o, half):
        ref = i_slot(o, half, 0)
        send(remote(ref, ref, z_send.at[o, half, 0], z_recv.at[o, half, 0], up, c))
        send(remote(ref, ref, z_send.at[o, half, 1], z_recv.at[o, half, 1], down, c))

    def shared(o):
        i_wait(i_slot(o, 0, 0), p1_recv.at[o])

    def shared_xl(o):
        i_wait(i_slot(o, 1, 0), xl_recv.at[o, 0])

    def one_end(o, half):
        d = 3 if half == 0 else 1
        ref = i_slot(o, half, d)
        i_wait(ref, z_recv.at[o, half, half])
        send(remote(ref, ref, z2_send.at[o, half], z2_recv.at[o, half], up if half == 0 else down, c))
        if o in LATE_XL:
            to_xl(o, d)

    def other_end(o, half):
        d = 1 if half == 0 else 3
        i_wait(i_slot(o, half, d), z_recv.at[o, half, 1 - half])
        if o in LATE_XL:
            to_xl(o, d)

    def far_end(o, half):
        i_wait(i_slot(o, half, 2), z2_recv.at[o, half])
        if o in LATE_XL:
            to_xl(o, 2)

    def rest_of(o):
        if o in LATE_XL:
            for d in (1, 3, 2):
                i_wait(i_slot(o, 1, d), xl_recv.at[o, d])
        else:
            other_end(o, 0)
            far_end(o, 0)
            other_end(o, 1)
            far_end(o, 1)

    def line(first, count):
        at = first // 128
        parts = [sector[pl.ds(jnp.minimum(at + i, 49), 1), :] for i in range(count)]
        flat = jnp.broadcast_to(jnp.concatenate(parts, axis=1), (8, 128 * count))
        return pltpu.roll(flat, 128 * count - (first - at * 128), axis=1)
    sec_cols = line(r * TILE, 8)[0:1, :NPAD]
    sec_rows[...] = jnp.broadcast_to(line(c * KB, 5)[0:1, :512], (128, 512)).astype(F32).T
    sec_cols = sec_cols.astype(F32)

    own_half = s_buf.at[pl.ds(pl.multiple_of(k * KB, 16), KB), :]
    mate_half = s_buf.at[pl.ds(pl.multiple_of((1 - k) * KB, 16), KB), :]

    def assemble():
        own1.wait()
        remote(sendbuf.at[pl.ds(0, 127)], fin.at[pl.ds(0, 127)], s1_send, s1_recv, r, c).wait_recv()

        def put(a, carry):
            for b in range(16):
                x_buf[pl.ds(pl.multiple_of(32 * a, 32), 32), pl.ds(128 * b, 128)] = fin[owner[16 * a + b]]
            return carry
        lax.fori_loop(0, 8, put, 0)
        m_i = lax.broadcasted_iota(jnp.int32, (KB, 256), 0)
        n_i = lax.broadcasted_iota(jnp.int32, (KB, 256), 1)
        blk = (m_i * 1311) >> 16
        inner = m_i - 50 * blk
        f1 = jnp.where((inner < 32) & (n_i == 32 * blk + inner), 1.0, 0.0).astype(BF)
        f2 = jnp.where((inner >= 32) & (n_i == 32 * blk + inner - 32), 1.0, 0.0).astype(BF)
        for n0, nw, k0, kw in ((0, 256, 0, 768), (256, 256, 640, 768), (512, 256, 1280, 768), (768, 128, 1920, 128)):
            x = x_buf[:, pl.ds(k0, kw)]
            y1 = jnp.dot(x, e1[pl.ds(k0, kw), pl.ds(n0, nw)], preferred_element_type=F32).astype(BF)
            y2 = jnp.dot(x, e2[pl.ds(k0, kw), pl.ds(n0, nw)], preferred_element_type=F32).astype(BF)
            part = jnp.dot(f1, y1, preferred_element_type=F32) + jnp.dot(f2, y2, preferred_element_type=F32)
            s_buf[pl.ds(pl.multiple_of(k * KB, 16), KB), pl.ds(n0, nw)] = part.astype(BF)
        send(remote(own_half, own_half, ex_send.at[0], ex_recv.at[0], r, mate))

    yup, ydown = col(xh, y + 1, k), col(xh, y + 3, k)

    def a_rows(cc, rows):
        return arecv.at[cc, pl.ds(rows[0], rows[1]), :]

    def a_send_to(cc, i, j, dest, rows=WHOLE):
        ref = a_rows(cc, rows)
        send(remote(ref, ref, a_send.at[i], a_recv.at[j], r, dest))

    def a_wait(cc, j, rows=WHOLE):
        ref = a_rows(cc, rows)
        remote(ref, ref, a_send.at[0], a_recv.at[j], r, c).wait_recv()

    def xy(dxh, dy, kk):
        return col(xh + dxh - 2 * xh * dxh, y + dy + 4, kk)

    def complete():
        remote(mate_half, mate_half, ex_send.at[0], ex_recv.at[0], r, c).wait_recv()

        def turn(i, carry):
            at = pl.ds(pl.multiple_of(i * 128, 128), 128)
            st_buf[:, at] = s_buf[at, pl.ds(pl.multiple_of(k * MAIN, 128), 512)].T
            return carry
        lax.fori_loop(0, 7, turn, 0)

        def choose(i, carry):
            row0 = pl.multiple_of(i * 80, 16)
            straight = s_buf[pl.ds(pl.multiple_of(k * KB + row0, 16), 80), :]
            flipped = st_buf[pl.ds(pl.multiple_of(16 * k + row0, 16), 80), :]
            g_k = lax.broadcasted_iota(jnp.int32, (80, NPAD), 0) + (c * KB + row0)
            g_n = lax.broadcasted_iota(jnp.int32, (80, NPAD), 1) + r * TILE
            tile = jnp.where(g_k <= g_n, straight.astype(F32), flipped.astype(F32))
            tile = jnp.where(sec_rows[pl.ds(row0, 80), 0:1] == sec_cols, tile, 0.0)
            arecv[c, pl.ds(row0, 80), :] = tile[:, :NMAIN].astype(BF)
            tail[pl.ds(row0, 80), :] = tile[:, NMAIN:]
            return carry
        lax.fori_loop(0, 5, choose, 0)
        arecv[c, pl.ds(KB, 32), pl.ds(0, 512)] = tail[...].T[:32].astype(BF)
        arecv[c, pl.ds(KB, 32), pl.ds(512, 256)] = jnp.zeros((32, 256), BF)
        arecv[c, pl.ds(KB, 16), pl.ds(512, 128)] = tail[pl.ds(MAIN, 16), :].astype(BF)
        for i, rows in enumerate(CUTS_X):
            a_send_to(c, X_SEMS[i][0], X_SEMS[i][1], cross_c, rows=rows)
        a_send_to(c, 0, 1, yup)
        a_send_to(c, 1, 2, ydown)
        a_send_to(c, 3, 8, mate)

    def from_x():
        for i, rows in enumerate(CUTS_X):
            a_wait(cross_c, X_SEMS[i][1], rows)
        a_send_to(cross_c, 4, 3, yup)
        a_send_to(cross_c, 5, 4, ydown)
        a_send_to(cross_c, 6, 9, mate)

    def from_y(dxh, dy, j, on, to_mate):
        cc = xy(dxh, dy, k)
        a_wait(cc, j)
        i, j2, dest, rows = on
        a_send_to(cc, i, j2, dest, rows=rows)
        a_send_to(cc, *to_mate, mate)

    def from_y2(dxh, low, high, to_mate):
        cc = xy(dxh, 2, k)
        a_wait(cc, low, LOW)
        a_wait(cc, high, HIGH)
        a_send_to(cc, *to_mate, mate)

    def product(dxh, dy, n, first):
        c0, c1 = xy(dxh, dy, 0), xy(dxh, dy, 1)

        def add(at, part):
            if first:
                acc[:, at] = part
            else:
                acc[:, at] += part

        left = jnp.concatenate([irecv[c0], irecv[c1]], axis=1)
        if n < 3:
            at = pl.ds(n * 256, 256)
            right = jnp.concatenate([arecv[c0, pl.ds(0, MAIN), at], arecv[c1, pl.ds(0, MAIN), at]], axis=0)
            add(at, jnp.dot(left, right, preferred_element_type=F32))
        else:
            side = pl.ds(KB, 32)
            right = jnp.concatenate([arecv[c0, side, pl.ds(0, MAIN)], arecv[c1, side, pl.ds(0, MAIN)]], axis=1)
            add(pl.ds(NMAIN, 32), lax.dot_general(left, right, (((1,), (1,)), ((), ())), preferred_element_type=F32))

    def whole(cc, sem):
        ref = irecv.at[cc]
        remote(ref, ref, full_send.at[0], full_recv.at[sem], r, c).wait_recv()

    def multiply(i, n, first):
        dxh, dy, j = ((0, 0, 8), (1, 0, 9), (0, -1, 10), (0, 1, 11), (1, 1, 12), (1, -1, 13), (0, 2, 14), (1, 2, 15))[i]
        if n > 0:
            product(dxh, dy, n, first)
            return
        if i == 0:
            whole(mate, 0)
        elif i == 1:
            whole(xy(1, 0, 0), 1)
            whole(xy(1, 0, 1), 2)
        else:
            rest_of(dxh * 3 + {-1: 0, 1: 1, 2: 2}[dy])
        a_wait(xy(dxh, dy, 1 - k), j)
        product(dxh, dy, n, first)

    steps = {"F": send_fulls, "F0": prepare, "E1": assemble, "E2": complete, "C": from_x}
    for i in range(3):
        steps["S%d" % i] = functools.partial(send_p1, i)
    for o in range(6):
        steps["P%d" % o] = functools.partial(shared, o)
        steps["X%d" % o] = functools.partial(shared_xl, o)
        steps["Y%d" % o] = functools.partial(to_xl, o, 0)
        steps["ZA%d" % o] = functools.partial(both_ways, o, 0)
        steps["ZB%d" % o] = functools.partial(both_ways, o, 1)
        for half in range(2):
            steps["U%d%d" % (o, half)] = functools.partial(one_end, o, half)
            steps["V%d%d" % (o, half)] = functools.partial(other_end, o, half)
            steps["W%d%d" % (o, half)] = functools.partial(far_end, o, half)
    steps["L"] = functools.partial(from_y, 0, -1, 1, (7, 5, yup, LOW), (8, 10))
    steps["H"] = functools.partial(from_y, 0, 1, 2, (15, 16, ydown, HIGH), (9, 11))
    steps["G"] = functools.partial(from_y, 1, 1, 4, (10, 6, ydown, HIGH), (11, 12))
    steps["J"] = functools.partial(from_y, 1, -1, 3, (16, 17, yup, LOW), (12, 13))
    steps["Q"] = functools.partial(from_y2, 0, 5, 16, (13, 14))
    steps["R"] = functools.partial(from_y2, 1, 17, 6, (14, 15))
    for name in ORDER:
        if name[0] == "M":
            multiply(int(name[1]), int(name[2]), name[1] == "0")
        else:
            steps[name]()

    for cc in range(16):
        arem[pl.ds(16 * cc, 16), pl.ds(0, NMAIN)] = arecv[cc, pl.ds(MAIN, REM), :]
        arem[pl.ds(16 * cc, 16), pl.ds(NMAIN, 128)] = arecv[cc, pl.ds(KB, 16), pl.ds(512, 128)]
        for q in range(4):
            l_buf[q, pl.ds(16 * cc, 16), :] = irecv[cc, pl.ds(q * SLOT + PIECE, REM), pl.ds(0, 256)]
    for q, (skip, row0) in enumerate(((0, 0), (16, 208), (16, 400), (0, 592))):
        part = lax.dot_general(l_buf[q], arem[...], (((0,), (0,)), ((), ())), preferred_element_type=F32)
        rows = PIECE - skip
        total = acc[pl.ds(q * SLOT + skip, rows), pl.ds(0, TILE)] + part[skip:PIECE, :TILE]
        out[pl.ds(row0, rows), :] = total.astype(BF)

    for cp in sends:
        cp.wait_send()
    remote(sendbuf.at[pl.ds(0, 127)], fin.at[pl.ds(0, 127)], s1_send, s1_recv, r, c).wait_send()


def slot_constants():
    table = np.zeros((128, 128), np.int32)
    for cls in range(128):
        a, b = cls // 16, cls % 16
        blocks = [(a + 8 * t, b + 16 * u) for t in range(16) for u in range(8) if a + 8 * t <= b + 16 * u]
        place = {block: i for i, block in enumerate(blocks)}
        for n in range(128):
            rr, cc = n // 16, n % 16
            lo, hi, h = min(rr, cc // 2), max(rr, cc // 2), cc % 2
            table[cls, n] = place.get((a + 8 * (2 * lo + h), b + 16 * hi), 0)
    return table


def slot_table(owner_map, me):
    return jnp.sum(jnp.where((owner_map == me)[:, None], jnp.asarray(slot_constants()), 0), axis=0)


def body(integrals, packed_store, pair_sector, owner_map):
    slots = slot_table(owner_map, lax.axis_index("row") * 16 + lax.axis_index("col"))
    packed = (jnp.pad(packed_store[:, :32], ((0, 0), (0, 0), (0, 78)))
              + jnp.pad(packed_store[:, 32:], ((0, 0), (0, 14), (50, 28))))
    dma = pltpu.SemaphoreType.DMA
    vm = lambda *s: pltpu.VMEM(s, BF)
    return pl.pallas_call(
        kernel,
        out_shape=jax.ShapeDtypeStruct((TILE, TILE), BF),
        in_specs=[pl.BlockSpec(memory_space=pltpu.SMEM)] * 2 + [pl.BlockSpec(memory_space=pl.ANY)]
        + [pl.BlockSpec(memory_space=pltpu.VMEM)] * 2,
        out_specs=pl.BlockSpec(memory_space=pltpu.VMEM),
        scratch_shapes=[
            vm(128, 32, 128), vm(128, 32, 128),
            vm(6, KB, 384), vm(4, KB, 896), vm(6, SLOT, MAIN), vm(3, ROWS, MAIN), vm(16, ROWS, MAIN), vm(16, NROWS, NMAIN),
            vm(256, 2048), vm(2048, NPAD), vm(2048, NPAD), vm(NPAD, NPAD), vm(512, NPAD),
            pltpu.VMEM((ROWS, NPAD), F32), vm(4, 256, 256), vm(256, NPAD), pltpu.VMEM((512, 128), F32), pltpu.VMEM((512, 128), F32),
            pltpu.SemaphoreType.REGULAR, dma((6,)), dma((4,)), dma, dma, dma,
            dma((6,)), dma((6,)), dma((3,)), dma((3,)),
            dma((6, 2, 2)), dma((6, 2, 2)), dma((6, 2)), dma((6, 2)), dma((6, 4)), dma((6, 4)), dma((1,)), dma((1,)),
            dma((19,)), dma((20,)),
        ],
        compiler_params=pltpu.CompilerParams(collective_id=1, has_side_effects=True, vmem_limit_bytes=60 * 2**20),
        cost_estimate=pl.CostEstimate(flops=2 * 800 * 800 * 6400, bytes_accessed=20_000_000, transcendentals=0),
    )(slots, owner_map, integrals.T, packed, pair_sector.reshape(50, 128))


def solution(mesh):
    in_specs = (P(None, "col"), P(("row", "col"), None, None), P(), P())
    return jax.shard_map(body, mesh=mesh, in_specs=in_specs, out_specs=P("col", "row"), check_vma=False)
```
